256 devices in a mesh: mem: 32 (over y, z), pt: 8 (over x, core).
Axes of the slice: x: 4, y: 4, z: 8, core: 2. Of those that a mesh axis runs over, the one named last changes fastest.
Arguments:
- ensemble: bfloat16 [4, 64, 524288], P(None, 'mem', 'pt'), may hold values from -6 to 6
- obs_members: bfloat16 [64, 524288], P('mem', 'pt'), may hold values from -6 to 6
- obs_value: bfloat16 [524288], P('pt'), may hold values from -6 to 6
- obs_precision: bfloat16 [524288], P('pt'), may hold values from 0.25 to 4
- tapering: bfloat16 [8, 32, 8, 2048], P('pt', 'mem'), may hold values from 0.049804688 to 1
- routes: int32 [32, 8, 8, 1024], P('mem', 'pt'), may hold values from 0 to 2047, as said below
- block_slots: int32 [8, 32, 8, 2048], P('pt', 'mem'), may hold values from 0 to 8191, as said below
- block_counts: int32 [8, 32, 8], P('pt', 'mem'), may hold values from 512 to 2048, as said below
Outputs:
- analysis: bfloat16 [4, 64, 524288], P(None, 'mem', 'pt')
The draws below stay inside these ranges and needn't reach their ends.
Inputs may be any that keep to these rules, and one draw needn't show every extreme that they name: routes[m, q, p, :] are 1024 different rows among the 2048 rows of collector (q, m). block_slots[p, m, i, :] are 2048 different slots among the 8192 slots of pool (p, m). `block_counts`: some block has all 2048 slots live.
All inputs are finite; a program needn't handle non-finite values.
Results may differ from the reference program's by a relative error of at most 0.017.
Values may be sent and summed in bfloat16 or wider, within the bound.
No kernel may reach another device: no remote copies, remote signals or barrier semaphores. Data moves between devices by JAX's collectives and lax.ppermute only.
A program may use at most 64 MiB of HBM per device.

```python
import math
import jax
import jax.numpy as jnp
from jax import lax

K = 64
NF = 4
BLK = 256
NBD = 8
NOBS_DEV = 2048
CAP = 1024
OBS_BLK = 2048
NS_ITERS = 6
P_SIZE = 524288
NOBS = 524288
N_MEM = 32
N_PT = 8


def distinct_prefix(key, shape, pool_size, keep):
    scores = jax.random.randint(key, shape + (pool_size,), 0, 2 ** 30 // pool_size)
    scores = scores * pool_size + lax.broadcasted_iota(jnp.int32, scores.shape, len(shape))
    ordering = jnp.argsort(scores, axis=len(shape))
    return ordering[..., :keep].astype(jnp.int32)


def draw_routes(key, part):
    return distinct_prefix(jax.random.fold_in(key, 11), (N_MEM, N_PT, N_PT), NOBS_DEV, CAP)


def draw_block_slots(key, part):
    return distinct_prefix(jax.random.fold_in(key, 23), (N_PT, N_MEM, NBD), N_PT * CAP, OBS_BLK)


def draw_block_counts(key, part):
    drawn = jax.random.randint(jax.random.fold_in(key, 31), (N_PT, N_MEM, NBD), OBS_BLK // 4, OBS_BLK + 1)
    flattened = drawn.reshape(-1)
    chosen = jax.random.randint(jax.random.fold_in(key, 37), (), 0, flattened.shape[0])
    chosen_mask = lax.broadcasted_iota(jnp.int32, flattened.shape, 0) == chosen
    return jnp.where(chosen_mask, OBS_BLK, flattened).reshape(drawn.shape).astype(jnp.int32)


def block_scale(rng, dims, shards, low, top_value):
    loudness, own = 1.0, jax.random.fold_in(rng, 6)
    for axis_at, parts in shards:
        heights = jnp.exp(jax.random.uniform(jax.random.fold_in(own, axis_at), (parts,), jnp.float32, low / len(shards), top_value / len(shards)))
        loudness = loudness * jnp.repeat(heights, dims[axis_at] // parts).reshape([-1 if axis == axis_at else 1 for axis in range(len(dims))])
    return loudness


def normal_values(own_key, extent, width, limit, pieces=(), kind=jnp.bfloat16):
    values = jax.random.normal(own_key, extent, jnp.float32) * width
    if len(pieces) > 0:
        values = block_scale(own_key, extent, pieces, -0.22, 0.18) * values
    return jnp.clip(values, min=-limit, max=limit).astype(kind)


def setup_inputs(seed: int = 0) -> dict:
    keys = jax.random.split(jax.random.key(seed), 9)
    return {
        "ensemble": normal_values(keys[0], (NF, K, P_SIZE), 1.0, 6.0, ((1, 32), (2, 8))),
        "obs_members": normal_values(keys[1], (K, NOBS), 1.0, 6.0, ((0, 32), (1, 8))),
        "obs_value": normal_values(keys[2], (NOBS,), 1.0, 6.0, ((0, 8),)),
        "obs_precision": jnp.clip(jnp.exp(math.log(4.0) - 2.7725887 * jax.random.uniform(keys[3], (NOBS,), jnp.float32) ** block_scale(keys[3], (NOBS,), ((0, 8),), -0.2, 0.2)), 0.25, 4.0).astype(jnp.bfloat16),
        "tapering": jnp.clip(0.049804688 + 0.9501953 * jax.random.uniform(keys[4], (N_PT, N_MEM, NBD, OBS_BLK), jnp.float32) ** block_scale(keys[4], (N_PT, N_MEM, NBD, OBS_BLK), ((0, 8), (1, 32)), -0.2, 0.2), 0.049804688, 1.0).astype(jnp.bfloat16),
        "routes": draw_routes(jax.random.fold_in(keys[8], 71), 0),
        "block_slots": draw_block_slots(jax.random.fold_in(keys[8], 71), 0),
        "block_counts": draw_block_counts(jax.random.fold_in(keys[8], 71), 0),
    }


def block_weights(raw_obs, obs_meta, tapering, live_count):
    highest = lax.Precision.HIGHEST
    widened = raw_obs.astype(jnp.float32)
    obs_mean = lax.optimization_barrier(jnp.mean(widened, axis=0))
    perturbed = (widened - obs_mean).astype(jnp.bfloat16)
    position = lax.broadcasted_iota(jnp.int32, tapering.shape, 1)
    live_mask = (position < live_count[:, None]).astype(jnp.float32)
    weight = tapering.astype(jnp.float32) * obs_meta[1].astype(jnp.float32) * live_mask
    weighted = (perturbed.astype(jnp.float32) * weight).astype(jnp.bfloat16)
    innovation = obs_meta[0].astype(jnp.float32) - obs_mean
    gram_matrix = jnp.einsum('kbr,jbr->bkj', weighted.astype(jnp.float32), perturbed.astype(jnp.float32), precision=highest)
    members = raw_obs.shape[0]
    identity = jnp.eye(members, dtype=jnp.float32)
    system = (members - 1.0) * identity + 0.5 * (gram_matrix + jnp.swapaxes(gram_matrix, 1, 2))
    projected = jnp.einsum('kbr,br->bk', weighted.astype(jnp.float32), innovation, precision=highest)
    frobenius = jnp.sqrt(lax.optimization_barrier(jnp.sum(system * system, axis=(1, 2))))
    root_half = system / frobenius[:, None, None]
    root_inv = jnp.broadcast_to(identity, system.shape)
    for sweep in range(NS_ITERS):
        update = 1.5 * identity - 0.5 * jnp.einsum('bij,bjk->bik', root_inv, root_half, precision=highest)
        root_half = jnp.einsum('bij,bjk->bik', root_half, update, precision=highest)
        root_inv = jnp.einsum('bij,bjk->bik', update, root_inv, precision=highest)
    inverse_root = root_inv / jnp.sqrt(frobenius)[:, None, None]
    inner = jnp.einsum('bij,bj->bi', inverse_root, projected, precision=highest)
    mean_shift = jnp.einsum('bij,bj->bi', inverse_root, inner, precision=highest)
    return (math.sqrt(members - 1.0) * inverse_root + mean_shift[:, :, None]).astype(jnp.bfloat16)

def apply_weights(state_blocks, weights):
    widened = state_blocks.astype(jnp.float32)
    state_mean = lax.optimization_barrier(jnp.mean(widened, axis=1, keepdims=True))
    deviation = (widened - state_mean).astype(jnp.bfloat16)
    moved = jnp.einsum('fjbc,bjk->fkbc', deviation.astype(jnp.float32), weights.astype(jnp.float32), precision=lax.Precision.HIGHEST)
    return (state_mean + moved).astype(jnp.bfloat16)

def reference(ensemble, obs_members, obs_value, obs_precision, tapering, routes, block_slots, block_counts):
    fields, members, cell_count = ensemble.shape
    state_all = ensemble.reshape(fields, members, N_PT, N_MEM, NBD, BLK)
    observed = obs_members.reshape(members, N_PT, N_MEM, NOBS_DEV)
    obs_meta = jnp.stack([obs_value, obs_precision]).reshape(2, N_PT, N_MEM, NOBS_DEV)
    sources = jnp.arange(N_PT, dtype=jnp.int32)[:, None]

    def one_group(group_index):
        pt_index = group_index // N_MEM
        mem_index = group_index % N_MEM
        row_lists = routes[mem_index, :, pt_index, :]
        pool_members = observed[:, sources, mem_index, row_lists].reshape(members, N_PT * CAP)
        pool_meta = obs_meta[:, sources, mem_index, row_lists].reshape(2, N_PT * CAP)
        slot_index = block_slots[pt_index, mem_index]
        weights = block_weights(pool_members[:, slot_index], pool_meta[:, slot_index], tapering[pt_index, mem_index], block_counts[pt_index, mem_index])
        return apply_weights(state_all[:, :, pt_index, mem_index], weights)
    analysed = lax.map(one_group, jnp.arange(N_PT * N_MEM, dtype=jnp.int32))
    analysed = analysed.reshape(N_PT, N_MEM, fields, members, NBD, BLK)
    return jnp.transpose(analysed, (2, 3, 0, 1, 4, 5)).reshape(fields, members, cell_count)
```

```python
import functools
import math

import jax
import jax.numpy as jnp
from jax import lax
from jax.experimental import pallas as pl
from jax.experimental.pallas import tpu as pltpu
from jax.sharding import PartitionSpec as P

NS_ITERS = 6
LANES = 128
CHUNK = 256
F32 = jnp.float32
BF16 = jnp.bfloat16
NT = (((1,), (1,)), ((), ()))
TN = (((0,), (0,)), ((), ()))


def spread_kernel(slots_ref, taper_ref, counts_ref, route_hi_ref, route_lo_ref, precision_ref, out_ref, slot_ref, lhs_ref):
    blocks, width = slots_ref.shape
    sources, cap = route_hi_ref.shape
    slot_rows = sources * cap // LANES
    row_tiles = precision_ref.shape[0] // sources
    position = lax.broadcasted_iota(jnp.int32, (1, width), 1)
    hi_iota = lax.broadcasted_iota(jnp.int32, (slot_rows, width), 0)
    lo_iota = lax.broadcasted_iota(jnp.int32, (LANES, width), 0)
    for b in range(blocks):
        slots = slots_ref[b : b + 1, :]
        live = position < counts_ref[b]
        value = jnp.where(live, taper_ref[b : b + 1, :].astype(F32), 0.0)
        hi = jnp.where(hi_iota == (slots >> 7), value, 0.0).astype(BF16)
        lo = jnp.where(lo_iota == (slots & (LANES - 1)), 1.0, 0.0).astype(BF16)
        slot_ref[b] = lax.dot_general(hi, lo, NT, preferred_element_type=F32)
    tile_iota = lax.broadcasted_iota(jnp.int32, (row_tiles, cap), 0)
    lane_iota = lax.broadcasted_iota(jnp.int32, (LANES, cap), 0)
    parts = cap // LANES
    for q in range(sources):
        in_tile = tile_iota == route_hi_ref[q : q + 1, :]
        onehot = jnp.where(lane_iota == route_lo_ref[q : q + 1, :], 1.0, 0.0).astype(BF16)
        for b in range(blocks):
            for c in range(parts):
                row = slot_ref[b, q * parts + c : q * parts + c + 1, :]
                lhs_ref[b * row_tiles : (b + 1) * row_tiles, c * LANES : (c + 1) * LANES] = jnp.where(
                    in_tile[:, c * LANES : (c + 1) * LANES], row, 0.0
                ).astype(BF16)
        rows = lax.dot_general(lhs_ref[...], onehot, NT, preferred_element_type=F32)
        precision = precision_ref[q * row_tiles : (q + 1) * row_tiles, :].astype(F32)
        for b in range(blocks):
            out_ref[b, q * row_tiles : (q + 1) * row_tiles, :] = rows[b * row_tiles : (b + 1) * row_tiles] * precision


def spread_weights(slots, taper, counts, route_hi, route_lo, precision):
    blocks = slots.shape[0]
    sources, cap = route_hi.shape
    row_tiles = precision.shape[0] // sources
    vmem = pl.BlockSpec(memory_space=pltpu.VMEM)
    return pl.pallas_call(
        spread_kernel,
        out_shape=jax.ShapeDtypeStruct((blocks,) + precision.shape, F32),
        in_specs=[vmem, vmem, pl.BlockSpec(memory_space=pltpu.SMEM), vmem, vmem, vmem],
        out_specs=vmem,
        scratch_shapes=[
            pltpu.VMEM((blocks, sources * cap // LANES, LANES), F32),
            pltpu.VMEM((blocks * row_tiles, cap), BF16),
        ],
        compiler_params=pltpu.CompilerParams(vmem_limit_bytes=32 * 2**20),
        cost_estimate=pl.CostEstimate(flops=2 * 10**9, bytes_accessed=10**6, transcendentals=0),
        name="spread_weights",
    )(slots, taper, counts, route_hi, route_lo, precision)


def matmul(a, b):
    return lax.dot_general(
        a, b, (((1,), (0,)), ((), ())), preferred_element_type=F32, precision=lax.Precision.HIGHEST
    )


def solve_kernel(pool_ref, weight_ref, value_ref, out_ref, lhs_ref, rhs_ref, total_ref):
    q = pl.program_id(0)
    blocks = weight_ref.shape[0]
    _, members, rows = pool_ref.shape
    extra = rhs_ref.shape[0] - members
    extra_iota = lax.broadcasted_iota(jnp.int32, (extra, LANES), 0)
    for t in range(rows // LANES):
        span = slice(t * LANES, (t + 1) * LANES)
        widened = pool_ref[0, :, span].astype(F32)
        mean = jnp.sum(widened, axis=0, keepdims=True) / members
        perturbed = (widened - mean).astype(BF16)
        rhs_ref[:members, span] = perturbed
        innovation = value_ref[0, t : t + 1, :].astype(F32) - mean
        first = innovation.astype(BF16).astype(F32)
        rest = innovation - first
        second = rest.astype(BF16).astype(F32)
        third = rest - second
        rhs_ref[members:, span] = jnp.where(
            extra_iota == 0, first, jnp.where(extra_iota == 1, second, jnp.where(extra_iota == 2, third, 0.0))
        ).astype(BF16)
        wide = perturbed.astype(F32)
        for b in range(blocks):
            lhs_ref[b * members : (b + 1) * members, span] = (wide * weight_ref[b, t : t + 1, :]).astype(BF16)
    product = lax.dot_general(lhs_ref[...], rhs_ref[...], NT, preferred_element_type=F32)

    @pl.when(q == 0)
    def _():
        total_ref[...] = product

    @pl.when(q > 0)
    def _():
        total_ref[...] += product

    @pl.when(q == pl.num_programs(0) - 1)
    def _():
        row = lax.broadcasted_iota(jnp.int32, (members, members), 0)
        column = lax.broadcasted_iota(jnp.int32, (members, members), 1)
        identity = jnp.where(row == column, 1.0, 0.0)
        halves, inverses, scales = [], [], []
        for b in range(blocks):
            gram = total_ref[b * members : (b + 1) * members, :members]
            system = (members - 1.0) * identity + 0.5 * (gram + gram.T)
            frobenius = jnp.sqrt(jnp.sum(system * system, keepdims=True))
            halves.append(system / frobenius)
            inverses.append(identity)
            scales.append(jnp.sqrt(frobenius))
        for sweep in range(NS_ITERS):
            updates = [
                1.5 * identity - 0.5 * (matmul(inverses[b], halves[b]) if sweep else halves[b]) for b in range(blocks)
            ]
            if sweep < NS_ITERS - 1:
                halves = [matmul(halves[b], updates[b]) for b in range(blocks)]
            inverses = [matmul(updates[b], inverses[b]) if sweep else updates[b] for b in range(blocks)]
        for b in range(blocks):
            inverse_root = inverses[b] / scales[b]
            projected = jnp.sum(
                total_ref[b * members : (b + 1) * members, members : members + 3], axis=1, keepdims=True
            )
            inner = jnp.sum(inverse_root * projected, axis=0, keepdims=True)
            mean_shift = jnp.sum(inverse_root * inner, axis=1, keepdims=True)
            out_ref[b] = (math.sqrt(members - 1.0) * inverse_root + mean_shift).astype(BF16)


def solve_weights(pool, weight, value):
    sources, members, rows = pool.shape
    blocks = weight.shape[0]
    tiles = rows // LANES
    return pl.pallas_call(
        solve_kernel,
        grid=(sources,),
        out_shape=jax.ShapeDtypeStruct((blocks, members, members), BF16),
        in_specs=[
            pl.BlockSpec((1, members, rows), lambda q: (q, 0, 0)),
            pl.BlockSpec((blocks, tiles, LANES), lambda q: (0, q, 0)),
            pl.BlockSpec((1, tiles, LANES), lambda q: (q, 0, 0)),
        ],
        out_specs=pl.BlockSpec((blocks, members, members), lambda q: (0, 0, 0)),
        scratch_shapes=[
            pltpu.VMEM((blocks * members, rows), BF16),
            pltpu.VMEM((members + 16, rows), BF16),
            pltpu.VMEM((blocks * members, members + 16), F32),
        ],
        compiler_params=pltpu.CompilerParams(vmem_limit_bytes=32 * 2**20),
        cost_estimate=pl.CostEstimate(flops=10 * 10**9, bytes_accessed=3 * 10**6, transcendentals=0),
        name="solve_weights",
    )(pool, weight, value)


def apply_kernel(state_ref, weights_ref, out_ref):
    _, members, cells = state_ref.shape
    blocks = weights_ref.shape[0]
    size = cells // blocks
    for b in range(blocks):
        span = slice(b * size, (b + 1) * size)
        widened = state_ref[0, :, span].astype(F32)
        mean = jnp.sum(widened, axis=0, keepdims=True) / members
        deviation = (widened - mean).astype(BF16)
        moved = lax.dot_general(weights_ref[b], deviation, TN, preferred_element_type=F32)
        out_ref[0, :, span] = (mean + moved).astype(BF16)


def apply_weights(state, weights):
    fields, members, cells = state.shape
    return pl.pallas_call(
        apply_kernel,
        grid=(fields,),
        out_shape=jax.ShapeDtypeStruct(state.shape, BF16),
        in_specs=[
            pl.BlockSpec((1, members, cells), lambda f: (f, 0, 0)),
            pl.BlockSpec(weights.shape, lambda f: (0, 0, 0)),
        ],
        out_specs=pl.BlockSpec((1, members, cells), lambda f: (f, 0, 0)),
        compiler_params=pltpu.CompilerParams(vmem_limit_bytes=32 * 2**20),
        cost_estimate=pl.CostEstimate(flops=10**9, bytes_accessed=2 * 10**6, transcendentals=0),
        name="apply_weights",
    )(state, weights)


def local(
    ensemble, obs_members, obs_value, obs_precision, tapering, routes, block_slots, block_counts
):
    mem_count = lax.axis_size("mem")
    fields, local_members, local_cells = ensemble.shape
    per_device = obs_members.shape[1] // mem_count
    owned_cells = local_cells // mem_count
    members = local_members * mem_count

    split_obs = obs_members.reshape(local_members, mem_count, per_device)
    collected = lax.all_to_all(split_obs, "mem", split_axis=1, concat_axis=1, tiled=True)
    collected = jnp.swapaxes(collected, 0, 1).reshape(members, per_device)

    offset = lax.axis_index("mem") * per_device
    row_lists = routes[0, 0]
    targets, cap = row_lists.shape
    side = jnp.concatenate(
        [
            lax.dynamic_slice_in_dim(obs_value, offset, per_device, 0).reshape(-1, LANES),
            lax.dynamic_slice_in_dim(obs_precision, offset, per_device, 0).reshape(-1, LANES),
            (row_lists >> 7).astype(BF16).reshape(-1, LANES),
            (row_lists & (LANES - 1)).astype(BF16).reshape(-1, LANES),
        ],
        axis=0,
    )
    sides = lax.all_gather(side, "pt", axis=0, tiled=False)
    sources = sides.shape[0]
    tiles = per_device // LANES
    cap_tiles = cap // LANES
    me = lax.axis_index("pt")
    value = sides[:, :tiles]
    precision = sides[:, tiles : 2 * tiles].reshape(sources * tiles, LANES)
    route_hi = lax.dynamic_slice_in_dim(sides, 2 * tiles + me * cap_tiles, cap_tiles, 1)
    route_lo = lax.dynamic_slice_in_dim(sides, 2 * tiles + (targets + me) * cap_tiles, cap_tiles, 1)
    weight = spread_weights(
        block_slots[0, 0],
        tapering[0, 0],
        block_counts[0, 0],
        route_hi.reshape(sources, cap).astype(jnp.int32),
        route_lo.reshape(sources, cap).astype(jnp.int32),
        precision,
    )

    pool = lax.all_gather(collected, "pt", axis=0, tiled=False)
    weights = solve_weights(pool, weight, value)

    state = ensemble.reshape(fields, local_members, mem_count, owned_cells)
    state = jnp.transpose(state, (2, 0, 1, 3))
    state = lax.all_to_all(state, "mem", split_axis=0, concat_axis=0, tiled=True)
    state = jnp.transpose(state, (1, 0, 2, 3)).reshape(fields, members, owned_cells)
    analysed = apply_weights(state, weights)
    analysed = jnp.transpose(
        analysed.reshape(fields, mem_count, local_members, owned_cells), (1, 0, 2, 3)
    )
    returned = lax.all_to_all(analysed, "mem", split_axis=0, concat_axis=0, tiled=True)
    return jnp.transpose(returned, (1, 2, 0, 3)).reshape(ensemble.shape)


def solution(mesh):
    placed = (
        P(None, "mem", "pt"),
        P("mem", "pt"),
        P("pt"),
        P("pt"),
        P("pt", "mem", None, None),
        P("mem", "pt", None, None),
        P("pt", "mem", None, None),
        P("pt", "mem", None),
    )
    return jax.shard_map(
        local, mesh=mesh, in_specs=placed, out_specs=P(None, "mem", "pt"), check_vma=False
    )
```

```python
import functools
import math

import jax
import jax.numpy as jnp
from jax import lax
from jax.experimental import pallas as pl
from jax.experimental.pallas import tpu as pltpu
from jax.sharding import PartitionSpec as P

NS_ITERS = 6
LANES = 128
CHUNK = 256
F32 = jnp.float32
BF16 = jnp.bfloat16
NT = (((1,), (1,)), ((), ()))
TN = (((0,), (0,)), ((), ()))


def spread_kernel(slots_ref, taper_ref, counts_ref, route_hi_ref, route_lo_ref, precision_ref, out_ref, slot_ref, lhs_ref):
    blocks, width = slots_ref.shape
    sources, cap = route_hi_ref.shape
    slot_rows = sources * cap // LANES
    row_tiles = precision_ref.shape[0] // sources
    position = lax.broadcasted_iota(jnp.int32, (1, width), 1)
    hi_iota = lax.broadcasted_iota(jnp.int32, (slot_rows, width), 0)
    lo_iota = lax.broadcasted_iota(jnp.int32, (LANES, width), 0)
    for b in range(blocks):
        slots = slots_ref[b : b + 1, :]
        live = position < counts_ref[b]
        value = jnp.where(live, taper_ref[b : b + 1, :].astype(F32), 0.0)
        hi = jnp.where(hi_iota == (slots >> 7), value, 0.0).astype(BF16)
        lo = jnp.where(lo_iota == (slots & (LANES - 1)), 1.0, 0.0).astype(BF16)
        slot_ref[b] = lax.dot_general(hi, lo, NT, preferred_element_type=F32)
    tile_iota = lax.broadcasted_iota(jnp.int32, (row_tiles, cap), 0)
    lane_iota = lax.broadcasted_iota(jnp.int32, (LANES, cap), 0)
    parts = cap // LANES
    for q in range(sources):
        in_tile = tile_iota == route_hi_ref[q : q + 1, :]
        onehot = jnp.where(lane_iota == route_lo_ref[q : q + 1, :], 1.0, 0.0).astype(BF16)
        for b in range(blocks):
            for c in range(parts):
                row = slot_ref[b, q * parts + c : q * parts + c + 1, :]
                lhs_ref[b * row_tiles : (b + 1) * row_tiles, c * LANES : (c + 1) * LANES] = jnp.where(
                    in_tile[:, c * LANES : (c + 1) * LANES], row, 0.0
                ).astype(BF16)
        rows = lax.dot_general(lhs_ref[...], onehot, NT, preferred_element_type=F32)
        precision = precision_ref[q * row_tiles : (q + 1) * row_tiles, :].astype(F32)
        for b in range(blocks):
            out_ref[b, q * row_tiles : (q + 1) * row_tiles, :] = rows[b * row_tiles : (b + 1) * row_tiles] * precision


def spread_weights(slots, taper, counts, route_hi, route_lo, precision):
    blocks = slots.shape[0]
    sources, cap = route_hi.shape
    row_tiles = precision.shape[0] // sources
    vmem = pl.BlockSpec(memory_space=pltpu.VMEM)
    return pl.pallas_call(
        spread_kernel,
        out_shape=jax.ShapeDtypeStruct((blocks,) + precision.shape, F32),
        in_specs=[vmem, vmem, pl.BlockSpec(memory_space=pltpu.SMEM), vmem, vmem, vmem],
        out_specs=vmem,
        scratch_shapes=[
            pltpu.VMEM((blocks, sources * cap // LANES, LANES), F32),
            pltpu.VMEM((blocks * row_tiles, cap), BF16),
        ],
        compiler_params=pltpu.CompilerParams(vmem_limit_bytes=32 * 2**20),
        cost_estimate=pl.CostEstimate(flops=2 * 10**9, bytes_accessed=10**6, transcendentals=0),
        name="spread_weights",
    )(slots, taper, counts, route_hi, route_lo, precision)


def matmul(a, b):
    return lax.dot_general(
        a, b, (((1,), (0,)), ((), ())), preferred_element_type=F32, precision=lax.Precision.HIGHEST
    )


def solve_kernel(pool_ref, weight_ref, value_ref, out_ref, lhs_ref, rhs_ref, total_ref):
    q = pl.program_id(0)
    blocks = weight_ref.shape[0]
    _, members, rows = pool_ref.shape
    extra = rhs_ref.shape[0] - members
    extra_iota = lax.broadcasted_iota(jnp.int32, (extra, LANES), 0)
    for t in range(rows // LANES):
        span = slice(t * LANES, (t + 1) * LANES)
        widened = pool_ref[0, :, span].astype(F32)
        mean = jnp.sum(widened, axis=0, keepdims=True) / members
        perturbed = (widened - mean).astype(BF16)
        rhs_ref[:members, span] = perturbed
        innovation = value_ref[0, t : t + 1, :].astype(F32) - mean
        first = innovation.astype(BF16).astype(F32)
        rest = innovation - first
        second = rest.astype(BF16).astype(F32)
        third = rest - second
        rhs_ref[members:, span] = jnp.where(
            extra_iota == 0, first, jnp.where(extra_iota == 1, second, jnp.where(extra_iota == 2, third, 0.0))
        ).astype(BF16)
        wide = perturbed.astype(F32)
        for b in range(blocks):
            lhs_ref[b * members : (b + 1) * members, span] = (wide * weight_ref[b, t : t + 1, :]).astype(BF16)
    product = lax.dot_general(lhs_ref[...], rhs_ref[...], NT, preferred_element_type=F32)

    @pl.when(q == 0)
    def _():
        total_ref[...] = product

    @pl.when(q > 0)
    def _():
        total_ref[...] += product

    @pl.when(q == pl.num_programs(0) - 1)
    def _():
        row = lax.broadcasted_iota(jnp.int32, (members, members), 0)
        column = lax.broadcasted_iota(jnp.int32, (members, members), 1)
        identity = jnp.where(row == column, 1.0, 0.0)
        halves, inverses, scales = [], [], []
        for b in range(blocks):
            gram = total_ref[b * members : (b + 1) * members, :members]
            system = (members - 1.0) * identity + 0.5 * (gram + gram.T)
            frobenius = jnp.sqrt(jnp.sum(system * system, keepdims=True))
            halves.append(system / frobenius)
            inverses.append(identity)
            scales.append(jnp.sqrt(frobenius))
        for sweep in range(NS_ITERS):
            updates = [
                1.5 * identity - 0.5 * (matmul(inverses[b], halves[b]) if sweep else halves[b]) for b in range(blocks)
            ]
            if sweep < NS_ITERS - 1:
                halves = [matmul(halves[b], updates[b]) for b in range(blocks)]
            inverses = [matmul(updates[b], inverses[b]) if sweep else updates[b] for b in range(blocks)]
        for b in range(blocks):
            inverse_root = inverses[b] / scales[b]
            projected = jnp.sum(
                total_ref[b * members : (b + 1) * members, members : members + 3], axis=1, keepdims=True
            )
            inner = jnp.sum(inverse_root * projected, axis=0, keepdims=True)
            mean_shift = jnp.sum(inverse_root * inner, axis=1, keepdims=True)
            out_ref[b] = (math.sqrt(members - 1.0) * inverse_root + mean_shift).astype(BF16)


def solve_weights(pool, weight, value):
    sources, members, rows = pool.shape
    blocks = weight.shape[0]
    tiles = rows // LANES
    return pl.pallas_call(
        solve_kernel,
        grid=(sources,),
        out_shape=jax.ShapeDtypeStruct((blocks, members, members), BF16),
        in_specs=[
            pl.BlockSpec((1, members, rows), lambda q: (q, 0, 0)),
            pl.BlockSpec((blocks, tiles, LANES), lambda q: (0, q, 0)),
            pl.BlockSpec((1, tiles, LANES), lambda q: (q, 0, 0)),
        ],
        out_specs=pl.BlockSpec((blocks, members, members), lambda q: (0, 0, 0)),
        scratch_shapes=[
            pltpu.VMEM((blocks * members, rows), BF16),
            pltpu.VMEM((members + 16, rows), BF16),
            pltpu.VMEM((blocks * members, members + 16), F32),
        ],
        compiler_params=pltpu.CompilerParams(vmem_limit_bytes=32 * 2**20),
        cost_estimate=pl.CostEstimate(flops=10 * 10**9, bytes_accessed=3 * 10**6, transcendentals=0),
        name="solve_weights",
    )(pool, weight, value)


def apply_kernel(state_ref, weights_ref, out_ref):
    _, members, cells = state_ref.shape
    blocks = weights_ref.shape[0]
    size = cells // blocks
    for b in range(blocks):
        span = slice(b * size, (b + 1) * size)
        widened = state_ref[0, :, span].astype(F32)
        mean = jnp.sum(widened, axis=0, keepdims=True) / members
        deviation = (widened - mean).astype(BF16)
        moved = lax.dot_general(weights_ref[b], deviation, TN, preferred_element_type=F32)
        out_ref[0, :, span] = (mean + moved).astype(BF16)


def apply_weights(state, weights):
    fields, members, cells = state.shape
    return pl.pallas_call(
        apply_kernel,
        grid=(fields,),
        out_shape=jax.ShapeDtypeStruct(state.shape, BF16),
        in_specs=[
            pl.BlockSpec((1, members, cells), lambda f: (f, 0, 0)),
            pl.BlockSpec(weights.shape, lambda f: (0, 0, 0)),
        ],
        out_specs=pl.BlockSpec((1, members, cells), lambda f: (f, 0, 0)),
        compiler_params=pltpu.CompilerParams(vmem_limit_bytes=32 * 2**20),
        cost_estimate=pl.CostEstimate(flops=10**9, bytes_accessed=2 * 10**6, transcendentals=0),
        name="apply_weights",
    )(state, weights)


def fence_kernel(*refs):
    del refs


def fence(array, *before):
    anywhere = pl.BlockSpec(memory_space=pl.ANY)
    return pl.pallas_call(
        fence_kernel,
        out_shape=jax.ShapeDtypeStruct(array.shape, array.dtype),
        in_specs=[anywhere] * (1 + len(before)),
        out_specs=anywhere,
        input_output_aliases={0: 0},
        compiler_params=pltpu.CompilerParams(vmem_limit_bytes=2**17),
        name="fence",
    )(array, *before)


def local(
    ensemble, obs_members, obs_value, obs_precision, tapering, routes, block_slots, block_counts
):
    mem_count = lax.axis_size("mem")
    fields, local_members, local_cells = ensemble.shape
    per_device = obs_members.shape[1] // mem_count
    owned_cells = local_cells // mem_count
    members = local_members * mem_count

    split_obs = obs_members.reshape(local_members, mem_count, per_device)
    collected = lax.all_to_all(split_obs, "mem", split_axis=1, concat_axis=1, tiled=True)
    collected = jnp.swapaxes(collected, 0, 1)

    offset = lax.axis_index("mem") * per_device
    row_lists = routes[0, 0]
    targets, cap = row_lists.shape
    side = jnp.concatenate(
        [
            lax.dynamic_slice_in_dim(obs_value, offset, per_device, 0).reshape(-1, LANES),
            lax.dynamic_slice_in_dim(obs_precision, offset, per_device, 0).reshape(-1, LANES),
            (row_lists >> 7).astype(BF16).reshape(-1, LANES),
            (row_lists & (LANES - 1)).astype(BF16).reshape(-1, LANES),
        ],
        axis=0,
    )
    sides = lax.all_gather(side, "pt", axis=0, tiled=False)
    sources = sides.shape[0]
    tiles = per_device // LANES
    cap_tiles = cap // LANES
    me = lax.axis_index("pt")
    value = sides[:, :tiles]
    precision = sides[:, tiles : 2 * tiles].reshape(sources * tiles, LANES)
    route_hi = lax.dynamic_slice_in_dim(sides, 2 * tiles + me * cap_tiles, cap_tiles, 1)
    route_lo = lax.dynamic_slice_in_dim(sides, 2 * tiles + (targets + me) * cap_tiles, cap_tiles, 1)
    weight = spread_weights(
        block_slots[0, 0],
        tapering[0, 0],
        block_counts[0, 0],
        route_hi.reshape(sources, cap).astype(jnp.int32),
        route_lo.reshape(sources, cap).astype(jnp.int32),
        precision,
    )

    collected = fence(collected, weight).reshape(members, per_device)
    pool = lax.all_gather(collected, "pt", axis=0, tiled=False)
    weights = solve_weights(pool, weight, value)

    state = ensemble.reshape(fields, local_members, mem_count, owned_cells)
    state = lax.all_to_all(state, "mem", split_axis=2, concat_axis=2, tiled=True)
    state = fence(jnp.transpose(state, (2, 0, 1, 3)), weights)
    state = jnp.transpose(state, (1, 0, 2, 3)).reshape(fields, members, owned_cells)
    analysed = apply_weights(state, weights)
    analysed = jnp.transpose(
        analysed.reshape(fields, mem_count, local_members, owned_cells), (1, 0, 2, 3)
    )
    returned = lax.all_to_all(analysed, "mem", split_axis=0, concat_axis=0, tiled=True)
    return jnp.transpose(returned, (1, 2, 0, 3)).reshape(ensemble.shape)


def solution(mesh):
    placed = (
        P(None, "mem", "pt"),
        P("mem", "pt"),
        P("pt"),
        P("pt"),
        P("pt", "mem", None, None),
        P("mem", "pt", None, None),
        P("pt", "mem", None, None),
        P("pt", "mem", None),
    )
    return jax.shard_map(
        local, mesh=mesh, in_specs=placed, out_specs=P(None, "mem", "pt"), check_vma=False
    )
```

```python
import functools
import math

import jax
import jax.numpy as jnp
from jax import lax
from jax.experimental import pallas as pl
from jax.experimental.pallas import tpu as pltpu
from jax.sharding import PartitionSpec as P

NS_ITERS = 6
LANES = 128
CHUNK = 256
SIDE_ROWS = 512
F32 = jnp.float32
BF16 = jnp.bfloat16
NN = (((1,), (0,)), ((), ()))
NT = (((1,), (1,)), ((), ()))
TN = (((0,), (0,)), ((), ()))


def spread_kernel(slots_ref, taper_ref, counts_ref, route_hi_ref, route_lo_ref, precision_ref, out_ref, slot_ref, lhs_ref):
    blocks, width = slots_ref.shape
    sources, cap = route_hi_ref.shape
    slot_rows = sources * cap // LANES
    row_tiles = precision_ref.shape[0] // sources
    position = lax.broadcasted_iota(jnp.int32, (1, width), 1)
    hi_iota = lax.broadcasted_iota(jnp.int32, (slot_rows, width), 0)
    lo_iota = lax.broadcasted_iota(jnp.int32, (LANES, width), 0)
    for b in range(blocks):
        slots = slots_ref[b : b + 1, :]
        live = position < counts_ref[b]
        value = jnp.where(live, taper_ref[b : b + 1, :].astype(F32), 0.0)
        hi = jnp.where(hi_iota == (slots >> 7), value, 0.0).astype(BF16)
        lo = jnp.where(lo_iota == (slots & (LANES - 1)), 1.0, 0.0).astype(BF16)
        slot_ref[b] = lax.dot_general(hi, lo, NT, preferred_element_type=F32)
    tile_iota = lax.broadcasted_iota(jnp.int32, (row_tiles, cap), 0)
    lane_iota = lax.broadcasted_iota(jnp.int32, (LANES, cap), 0)
    parts = cap // LANES
    for q in range(sources):
        in_tile = tile_iota == route_hi_ref[q : q + 1, :]
        onehot = jnp.where(lane_iota == route_lo_ref[q : q + 1, :], 1.0, 0.0).astype(BF16)
        for b in range(blocks):
            for c in range(parts):
                row = slot_ref[b, q * parts + c : q * parts + c + 1, :]
                lhs_ref[b * row_tiles : (b + 1) * row_tiles, c * LANES : (c + 1) * LANES] = jnp.where(
                    in_tile[:, c * LANES : (c + 1) * LANES], row, 0.0
                ).astype(BF16)
        rows = lax.dot_general(lhs_ref[...], onehot, NT, preferred_element_type=F32)
        precision = precision_ref[q * row_tiles : (q + 1) * row_tiles, :].astype(F32)
        for b in range(blocks):
            out_ref[b, q * row_tiles : (q + 1) * row_tiles, :] = rows[b * row_tiles : (b + 1) * row_tiles] * precision


def spread_weights(slots, taper, counts, route_hi, route_lo, precision):
    blocks = slots.shape[0]
    sources, cap = route_hi.shape
    row_tiles = precision.shape[0] // sources
    vmem = pl.BlockSpec(memory_space=pltpu.VMEM)
    return pl.pallas_call(
        spread_kernel,
        out_shape=jax.ShapeDtypeStruct((blocks,) + precision.shape, F32),
        in_specs=[vmem, vmem, pl.BlockSpec(memory_space=pltpu.SMEM), vmem, vmem, vmem],
        out_specs=vmem,
        scratch_shapes=[
            pltpu.VMEM((blocks, sources * cap // LANES, LANES), F32),
            pltpu.VMEM((blocks * row_tiles, cap), BF16),
        ],
        compiler_params=pltpu.CompilerParams(vmem_limit_bytes=32 * 2**20),
        cost_estimate=pl.CostEstimate(flops=2 * 10**9, bytes_accessed=10**6, transcendentals=0),
        name="spread_weights",
    )(slots, taper, counts, route_hi, route_lo, precision)


def halves_of(x):
    high = x.astype(BF16)
    return high, (x - high.astype(F32)).astype(BF16)


def product(a, b):
    a_high, a_low = halves_of(a)
    b_high, b_low = halves_of(b)
    return lax.dot_general(
        jnp.concatenate([a_high, a_high, a_low], axis=1),
        jnp.concatenate([b_high, b_low, b_high], axis=0),
        NN,
        preferred_element_type=F32,
    )


def solve_kernel(pool_ref, weight_ref, value_ref, out_ref, held_ref, total_ref, sems, *parts):
    q = pl.program_id(0)
    sources, members, rows = held_ref.shape
    blocks = weight_ref.shape[0]
    twice = 2 * members
    lhs_refs, rhs_refs = parts[0::2], parts[1::2]
    size = lhs_refs[0].shape[1]
    extra = rhs_refs[0].shape[0] - twice

    def arrival(source):
        return pltpu.make_async_copy(pool_ref.at[source], held_ref.at[source], sems.at[source])

    @pl.when(q == 0)
    def _():
        for source in range(sources):
            arrival(source).start()

    arrival(q).wait()
    extra_iota = lax.broadcasted_iota(jnp.int32, (extra, LANES), 0)
    added = None
    for part, (lhs_ref, rhs_ref) in enumerate(zip(lhs_refs, rhs_refs, strict=True)):
        for u in range(size // LANES):
            t = part * (size // LANES) + u
            to = slice(u * LANES, (u + 1) * LANES)
            widened = held_ref[q, :, t * LANES : (t + 1) * LANES].astype(F32)
            mean = jnp.sum(widened, axis=0, keepdims=True) / members
            perturbed = (widened - mean).astype(BF16)
            rhs_ref[:members, to] = perturbed
            rhs_ref[members:twice, to] = perturbed
            innovation = value_ref[0, t : t + 1, :].astype(F32) - mean
            first = innovation.astype(BF16).astype(F32)
            rest = innovation - first
            second = rest.astype(BF16).astype(F32)
            third = rest - second
            rhs_ref[twice:, to] = jnp.where(
                extra_iota == 0, first, jnp.where(extra_iota == 1, second, jnp.where(extra_iota == 2, third, 0.0))
            ).astype(BF16)
            wide = perturbed.astype(F32)
            for b in range(blocks):
                lhs_ref[b * members : (b + 1) * members, to] = (wide * weight_ref[b, t : t + 1, :]).astype(BF16)
        term = lax.dot_general(lhs_ref[...], rhs_ref[...], NT, preferred_element_type=F32)
        added = term if added is None else added + term

    @pl.when(q == 0)
    def _():
        total_ref[...] = added

    @pl.when(q > 0)
    def _():
        total_ref[...] += added

    @pl.when(q == pl.num_programs(0) - 1)
    def _():
        row = lax.broadcasted_iota(jnp.int32, (twice, twice), 0)
        column = lax.broadcasted_iota(jnp.int32, (twice, twice), 1)
        identity = jnp.where(row == column, 1.0, 0.0)
        same = (row < members) == (column < members)
        upper = lax.broadcasted_iota(jnp.int32, (twice, 1), 0) < members
        pairs = range(blocks // 2)
        halves, scales = [], []
        for p in pairs:
            gram = jnp.where(same, total_ref[p * twice : (p + 1) * twice, :twice], 0.0)
            system = (members - 1.0) * identity + 0.5 * (gram + gram.T)
            squares = jnp.sum(system * system, axis=1, keepdims=True)
            frobenius = jnp.sqrt(
                jnp.where(
                    upper,
                    jnp.sum(jnp.where(upper, squares, 0.0), keepdims=True),
                    jnp.sum(jnp.where(upper, 0.0, squares), keepdims=True),
                )
            )
            halves.append(system / frobenius)
            scales.append(jnp.sqrt(frobenius))
        inverses = []
        for sweep in range(NS_ITERS):
            updates = [1.5 * identity - 0.5 * (product(inverses[p], halves[p]) if sweep else halves[p]) for p in pairs]
            if sweep == 0:
                halves = [product(halves[p], updates[p]) for p in pairs]
                inverses = updates
            elif sweep < NS_ITERS - 1:
                both = [product(jnp.concatenate([halves[p], inverses[p]], axis=0), updates[p]) for p in pairs]
                halves = [x[:twice] for x in both]
                inverses = [x[twice:] for x in both]
            else:
                inverses = [product(inverses[p], updates[p]) for p in pairs]
        for p in pairs:
            inverse_root = inverses[p] / scales[p]
            projected = jnp.sum(total_ref[p * twice : (p + 1) * twice, twice : twice + 3], axis=1, keepdims=True)
            inner = jnp.sum(inverse_root * projected, axis=0, keepdims=True)
            mean_shift = jnp.sum(inverse_root * inner, axis=1, keepdims=True)
            out_ref[p] = jnp.where(same, math.sqrt(members - 1.0) * inverse_root + mean_shift, 0.0).astype(BF16)


def solve_weights(pool, weight, value):
    sources, members, rows = pool.shape
    blocks = weight.shape[0]
    tiles = rows // LANES
    twice = 2 * members
    parts = []
    for _ in range(rows // CHUNK):
        parts += [pltpu.VMEM((blocks * members, CHUNK), BF16), pltpu.VMEM((twice + 16, CHUNK), BF16)]
    return pl.pallas_call(
        solve_kernel,
        grid=(sources,),
        out_shape=jax.ShapeDtypeStruct((blocks // 2, twice, twice), BF16),
        in_specs=[
            pl.BlockSpec(memory_space=pltpu.HBM),
            pl.BlockSpec((blocks, tiles, LANES), lambda q: (0, q, 0)),
            pl.BlockSpec((1, tiles, LANES), lambda q: (q, 0, 0)),
        ],
        out_specs=pl.BlockSpec((blocks // 2, twice, twice), lambda q: (0, 0, 0)),
        scratch_shapes=[
            pltpu.VMEM(pool.shape, BF16),
            pltpu.VMEM((blocks * members, twice + 16), F32),
            pltpu.SemaphoreType.DMA((sources,)),
        ]
        + parts,
        compiler_params=pltpu.CompilerParams(vmem_limit_bytes=58 * 2**20),
        cost_estimate=pl.CostEstimate(flops=10 * 10**9, bytes_accessed=3 * 10**6, transcendentals=0),
        name="solve_weights",
    )(pool, weight, value)


def apply_kernel(state_ref, weights_ref, out_ref):
    owners, fields, local_members, cells = state_ref.shape
    members = owners * local_members
    pairs, twice, _ = weights_ref.shape
    size = cells // (2 * pairs)
    for f in range(fields):
        for p in range(pairs):
            spans = [slice((2 * p + h) * size, (2 * p + h + 1) * size) for h in range(2)]
            means, deviations = [], []
            for span in spans:
                widened = state_ref[:, f, :, span].reshape(members, size).astype(F32)
                mean = jnp.sum(widened, axis=0, keepdims=True) / members
                means.append(mean)
                deviations.append((widened - mean).astype(BF16))
            moved = lax.dot_general(
                weights_ref[p], jnp.concatenate(deviations, axis=0), TN, preferred_element_type=F32
            )
            for h, span in enumerate(spans):
                out_ref[:, f, :, span] = (
                    (means[h] + moved[h * members : (h + 1) * members]).astype(BF16).reshape(owners, local_members, size)
                )


def apply_weights(state, weights):
    vmem = pl.BlockSpec(memory_space=pltpu.VMEM)
    return pl.pallas_call(
        apply_kernel,
        out_shape=jax.ShapeDtypeStruct(state.shape, BF16),
        in_specs=[vmem, vmem],
        out_specs=vmem,
        compiler_params=pltpu.CompilerParams(vmem_limit_bytes=32 * 2**20),
        cost_estimate=pl.CostEstimate(flops=10**9, bytes_accessed=2 * 10**6, transcendentals=0),
        name="apply_weights",
    )(state, weights)


def outward_kernel(flat_ref, owned_ref, sems):
    owners, _, _, cells = owned_ref.shape
    copies = [
        pltpu.make_async_copy(flat_ref.at[:, :, pl.ds(m * cells, cells)], owned_ref.at[m], sems.at[m])
        for m in range(owners)
    ]
    for copy in copies:
        copy.start()
    for copy in copies:
        copy.wait()


def homeward_kernel(owned_ref, flat_ref, sems):
    owners, _, _, cells = owned_ref.shape
    copies = [
        pltpu.make_async_copy(owned_ref.at[m], flat_ref.at[:, :, pl.ds(m * cells, cells)], sems.at[m])
        for m in range(owners)
    ]
    for copy in copies:
        copy.start()
    for copy in copies:
        copy.wait()


ANYWHERE = pl.BlockSpec(memory_space=pl.ANY)


def rearrange(kernel, array, shape, owners, name):
    return pl.pallas_call(
        kernel,
        out_shape=jax.ShapeDtypeStruct(shape, array.dtype),
        in_specs=[ANYWHERE],
        out_specs=ANYWHERE,
        scratch_shapes=[pltpu.SemaphoreType.DMA((owners,))],
        compiler_params=pltpu.CompilerParams(vmem_limit_bytes=2**17),
        name=name,
    )(array)


def fence_kernel(*refs):
    del refs


def fence(array, *before):
    return pl.pallas_call(
        fence_kernel,
        out_shape=jax.ShapeDtypeStruct(array.shape, array.dtype),
        in_specs=[ANYWHERE] * (1 + len(before)),
        out_specs=ANYWHERE,
        input_output_aliases={0: 0},
        compiler_params=pltpu.CompilerParams(vmem_limit_bytes=2**17),
        name="fence",
    )(array, *before)


def local(
    ensemble, obs_members, obs_value, obs_precision, tapering, routes, block_slots, block_counts
):
    mem_count = lax.axis_size("mem")
    fields, local_members, local_cells = ensemble.shape
    per_device = obs_members.shape[1] // mem_count
    owned_cells = local_cells // mem_count
    members = local_members * mem_count

    offset = lax.axis_index("mem") * per_device
    row_lists = routes[0, 0]
    targets, cap = row_lists.shape
    side = jnp.concatenate(
        [
            lax.dynamic_slice_in_dim(obs_value, offset, per_device, 0).reshape(-1, LANES),
            lax.dynamic_slice_in_dim(obs_precision, offset, per_device, 0).reshape(-1, LANES),
            (row_lists >> 7).astype(BF16).reshape(-1, LANES),
            (row_lists & (LANES - 1)).astype(BF16).reshape(-1, LANES),
        ],
        axis=0,
    )
    side = jnp.pad(side, ((0, max(SIDE_ROWS - side.shape[0], 0)), (0, 0)))
    sides = lax.all_gather(side, "pt", axis=0, tiled=False)
    sources = sides.shape[0]
    tiles = per_device // LANES
    cap_tiles = cap // LANES
    me = lax.axis_index("pt")
    value = sides[:, :tiles]
    precision = sides[:, tiles : 2 * tiles].reshape(sources * tiles, LANES)
    route_hi = lax.dynamic_slice_in_dim(sides, 2 * tiles + me * cap_tiles, cap_tiles, 1)
    route_lo = lax.dynamic_slice_in_dim(sides, 2 * tiles + (targets + me) * cap_tiles, cap_tiles, 1)
    weight = spread_weights(
        block_slots[0, 0],
        tapering[0, 0],
        block_counts[0, 0],
        route_hi.reshape(sources, cap).astype(jnp.int32),
        route_lo.reshape(sources, cap).astype(jnp.int32),
        precision,
    )

    split_obs = fence(obs_members, side).reshape(local_members, mem_count, per_device)
    collected = lax.all_to_all(split_obs, "mem", split_axis=1, concat_axis=1, tiled=True)
    state = rearrange(
        outward_kernel, ensemble, (mem_count, fields, local_members, owned_cells), mem_count, "outward"
    )
    collected = fence(jnp.swapaxes(collected, 0, 1), state).reshape(members, per_device)
    pool = lax.all_gather(collected, "pt", axis=0, tiled=False)
    weights = solve_weights(pool, weight, value)

    state = lax.all_to_all(state, "mem", split_axis=0, concat_axis=0, tiled=True)
    analysed = apply_weights(state, weights)
    returned = lax.all_to_all(analysed, "mem", split_axis=0, concat_axis=0, tiled=True)
    return rearrange(homeward_kernel, returned, ensemble.shape, mem_count, "homeward")


def solution(mesh):
    placed = (
        P(None, "mem", "pt"),
        P("mem", "pt"),
        P("pt"),
        P("pt"),
        P("pt", "mem", None, None),
        P("mem", "pt", None, None),
        P("pt", "mem", None, None),
        P("pt", "mem", None),
    )
    return jax.shard_map(
        local, mesh=mesh, in_specs=placed, out_specs=P(None, "mem", "pt"), check_vma=False
    )
```

```python
import functools
import math

import jax
import jax.numpy as jnp
from jax import lax
from jax.experimental import pallas as pl
from jax.experimental.pallas import tpu as pltpu
from jax.sharding import PartitionSpec as P

NS_ITERS = 6
LANES = 128
CHUNK = 256
F32 = jnp.float32
BF16 = jnp.bfloat16
NN = (((1,), (0,)), ((), ()))
NT = (((1,), (1,)), ((), ()))
TN = (((0,), (0,)), ((), ()))


def spread_kernel(me_ref, slots_ref, taper_ref, counts_ref, side_ref, weight_ref, value_ref, slot_ref, lhs_ref):
    blocks, width = slots_ref.shape
    sources, tiles, _ = value_ref.shape
    parts = (side_ref.shape[1] - 2 * tiles) // 2
    slot_rows = slot_ref.shape[1]
    position = lax.broadcasted_iota(jnp.int32, (1, width), 1)
    hi_iota = lax.broadcasted_iota(jnp.int32, (slot_rows, width), 0)
    lo_iota = lax.broadcasted_iota(jnp.int32, (LANES, width), 0)
    for b in range(blocks):
        slots = slots_ref[b : b + 1, :]
        live = position < counts_ref[b]
        value = jnp.where(live, taper_ref[b : b + 1, :].astype(F32), 0.0)
        hi = jnp.where(hi_iota == (slots >> 7), value, 0.0).astype(BF16)
        lo = jnp.where(lo_iota == (slots & (LANES - 1)), 1.0, 0.0).astype(BF16)
        slot_ref[b] = lax.dot_general(hi, lo, NT, preferred_element_type=F32)
    tile_iota = lax.broadcasted_iota(jnp.int32, (tiles, LANES), 0).astype(F32)
    lane_iota = lax.broadcasted_iota(jnp.int32, (LANES, LANES), 0).astype(F32)
    for q in range(sources):
        step = me_ref[0] ^ q
        value_ref[q] = side_ref[step, :tiles, :]
        precision = side_ref[step, tiles : 2 * tiles, :].astype(F32)
        route_hi = side_ref[step, 2 * tiles : 2 * tiles + parts, :].astype(F32)
        route_lo = side_ref[step, 2 * tiles + parts :, :].astype(F32)
        onehots = []
        for c in range(parts):
            onehots.append(jnp.where(lane_iota == route_lo[c : c + 1, :], 1.0, 0.0).astype(BF16))
            in_tile = tile_iota == route_hi[c : c + 1, :]
            for b in range(blocks):
                row = slot_ref[b, q * parts + c : q * parts + c + 1, :]
                lhs_ref[b * tiles : (b + 1) * tiles, c * LANES : (c + 1) * LANES] = jnp.where(
                    in_tile, row, 0.0
                ).astype(BF16)
        rows = lax.dot_general(
            lhs_ref[...], jnp.concatenate(onehots, axis=1), NT, preferred_element_type=F32
        )
        for b in range(blocks):
            weight_ref[q, b] = rows[b * tiles : (b + 1) * tiles] * precision


def spread_weights(me, slots, taper, counts, side, tiles):
    blocks = slots.shape[0]
    sources, rows, _ = side.shape
    parts = (rows - 2 * tiles) // 2
    vmem = pl.BlockSpec(memory_space=pltpu.VMEM)
    smem = pl.BlockSpec(memory_space=pltpu.SMEM)
    return pl.pallas_call(
        spread_kernel,
        out_shape=(
            jax.ShapeDtypeStruct((sources, blocks, tiles, LANES), F32),
            jax.ShapeDtypeStruct((sources, tiles, LANES), BF16),
        ),
        in_specs=[smem, vmem, vmem, smem, vmem],
        out_specs=(vmem, vmem),
        scratch_shapes=[
            pltpu.VMEM((blocks, sources * parts, LANES), F32),
            pltpu.VMEM((blocks * tiles, parts * LANES), BF16),
        ],
        compiler_params=pltpu.CompilerParams(vmem_limit_bytes=32 * 2**20),
        cost_estimate=pl.CostEstimate(flops=2 * 10**9, bytes_accessed=10**6, transcendentals=0),
        name="spread_weights",
    )(me, slots, taper, counts, side)


def halves_of(x):
    high = x.astype(BF16)
    return high, (x - high.astype(F32)).astype(BF16)


def product(a, b):
    a_high, a_low = halves_of(a)
    b_high, b_low = halves_of(b)
    return lax.dot_general(
        jnp.concatenate([a_high, a_high, a_low], axis=1),
        jnp.concatenate([b_high, b_low, b_high], axis=0),
        NN,
        preferred_element_type=F32,
    )


def solve_kernel(pool_ref, weight_ref, value_ref, out_ref, held_ref, total_ref, sems, *parts):
    sources, members, rows = held_ref.shape
    blocks = weight_ref.shape[1]
    twice = 2 * members
    lhs_refs, rhs_refs = parts[0::2], parts[1::2]
    size = lhs_refs[0].shape[1]
    extra = rhs_refs[0].shape[0] - twice

    def arrival(source):
        return pltpu.make_async_copy(pool_ref.at[source], held_ref.at[source], sems.at[source])

    for source in range(sources):
        arrival(source).start()
    total_ref[...] = jnp.zeros_like(total_ref)
    extra_iota = lax.broadcasted_iota(jnp.int32, (extra, LANES), 0)

    def add_source(q, carry):
        arrival(q).wait()
        added = None
        for part, (lhs_ref, rhs_ref) in enumerate(zip(lhs_refs, rhs_refs, strict=True)):
            for u in range(size // LANES):
                t = part * (size // LANES) + u
                to = slice(u * LANES, (u + 1) * LANES)
                widened = held_ref[q, :, t * LANES : (t + 1) * LANES].astype(F32)
                mean = jnp.sum(widened, axis=0, keepdims=True) / members
                perturbed = (widened - mean).astype(BF16)
                rhs_ref[:members, to] = perturbed
                rhs_ref[members:twice, to] = perturbed
                innovation = value_ref[q, t : t + 1, :].astype(F32) - mean
                first = innovation.astype(BF16).astype(F32)
                rest = innovation - first
                second = rest.astype(BF16).astype(F32)
                third = rest - second
                rhs_ref[twice:, to] = jnp.where(
                    extra_iota == 0, first, jnp.where(extra_iota == 1, second, jnp.where(extra_iota == 2, third, 0.0))
                ).astype(BF16)
                wide = perturbed.astype(F32)
                for b in range(blocks):
                    lhs_ref[b * members : (b + 1) * members, to] = (wide * weight_ref[q, b, t : t + 1, :]).astype(BF16)
            term = lax.dot_general(lhs_ref[...], rhs_ref[...], NT, preferred_element_type=F32)
            added = term if added is None else added + term
        total_ref[...] += added
        return carry

    lax.fori_loop(0, sources, add_source, 0)

    row = lax.broadcasted_iota(jnp.int32, (twice, twice), 0)
    column = lax.broadcasted_iota(jnp.int32, (twice, twice), 1)
    identity = jnp.where(row == column, 1.0, 0.0)
    same = (row < members) == (column < members)
    upper = lax.broadcasted_iota(jnp.int32, (twice, 1), 0) < members
    pairs = range(blocks // 2)
    halves, scales = [], []
    for p in pairs:
        gram = jnp.where(same, total_ref[p * twice : (p + 1) * twice, :twice], 0.0)
        system = (members - 1.0) * identity + 0.5 * (gram + gram.T)
        squares = jnp.sum(system * system, axis=1, keepdims=True)
        frobenius = jnp.sqrt(
            jnp.where(
                upper,
                jnp.sum(jnp.where(upper, squares, 0.0), keepdims=True),
                jnp.sum(jnp.where(upper, 0.0, squares), keepdims=True),
            )
        )
        halves.append(system / frobenius)
        scales.append(jnp.sqrt(frobenius))
    inverses = []
    for sweep in range(NS_ITERS):
        updates = [1.5 * identity - 0.5 * (product(inverses[p], halves[p]) if sweep else halves[p]) for p in pairs]
        if sweep == 0:
            halves = [product(halves[p], updates[p]) for p in pairs]
            inverses = updates
        elif sweep < NS_ITERS - 1:
            both = [product(jnp.concatenate([halves[p], inverses[p]], axis=0), updates[p]) for p in pairs]
            halves = [x[:twice] for x in both]
            inverses = [x[twice:] for x in both]
        else:
            inverses = [product(inverses[p], updates[p]) for p in pairs]
    for p in pairs:
        inverse_root = inverses[p] / scales[p]
        projected = jnp.sum(total_ref[p * twice : (p + 1) * twice, twice : twice + 3], axis=1, keepdims=True)
        inner = jnp.sum(inverse_root * projected, axis=0, keepdims=True)
        mean_shift = jnp.sum(inverse_root * inner, axis=1, keepdims=True)
        out_ref[p] = jnp.where(same, math.sqrt(members - 1.0) * inverse_root + mean_shift, 0.0).astype(BF16)


def solve_weights(pool, weight, value):
    sources, members, rows = pool.shape
    blocks = weight.shape[1]
    twice = 2 * members
    parts = []
    for _ in range(rows // CHUNK):
        parts += [pltpu.VMEM((blocks * members, CHUNK), BF16), pltpu.VMEM((twice + 16, CHUNK), BF16)]
    vmem = pl.BlockSpec(memory_space=pltpu.VMEM)
    return pl.pallas_call(
        solve_kernel,
        out_shape=jax.ShapeDtypeStruct((blocks // 2, twice, twice), BF16),
        in_specs=[pl.BlockSpec(memory_space=pltpu.HBM), vmem, vmem],
        out_specs=vmem,
        scratch_shapes=[
            pltpu.VMEM(pool.shape, BF16),
            pltpu.VMEM((blocks * members, twice + 16), F32),
            pltpu.SemaphoreType.DMA((sources,)),
        ]
        + parts,
        compiler_params=pltpu.CompilerParams(vmem_limit_bytes=53 * 2**20),
        cost_estimate=pl.CostEstimate(flops=10 * 10**9, bytes_accessed=3 * 10**6, transcendentals=0),
        name="solve_weights",
    )(pool, weight, value)


def apply_kernel(state_ref, weights_ref, out_ref):
    owners, fields, local_members, cells = state_ref.shape
    members = owners * local_members
    pairs, twice, _ = weights_ref.shape
    size = cells // (2 * pairs)
    for f in range(fields):
        for p in range(pairs):
            spans = [slice((2 * p + h) * size, (2 * p + h + 1) * size) for h in range(2)]
            means, deviations = [], []
            for span in spans:
                widened = state_ref[:, f, :, span].reshape(members, size).astype(F32)
                mean = jnp.sum(widened, axis=0, keepdims=True) / members
                means.append(mean)
                deviations.append((widened - mean).astype(BF16))
            moved = lax.dot_general(
                weights_ref[p], jnp.concatenate(deviations, axis=0), TN, preferred_element_type=F32
            )
            for h, span in enumerate(spans):
                out_ref[:, f, :, span] = (
                    (means[h] + moved[h * members : (h + 1) * members]).astype(BF16).reshape(owners, local_members, size)
                )


def apply_weights(state, weights):
    vmem = pl.BlockSpec(memory_space=pltpu.VMEM)
    return pl.pallas_call(
        apply_kernel,
        out_shape=jax.ShapeDtypeStruct(state.shape, BF16),
        in_specs=[vmem, vmem],
        out_specs=vmem,
        compiler_params=pltpu.CompilerParams(vmem_limit_bytes=32 * 2**20),
        cost_estimate=pl.CostEstimate(flops=10**9, bytes_accessed=2 * 10**6, transcendentals=0),
        name="apply_weights",
    )(state, weights)


def outward_kernel(flat_ref, owned_ref, sems):
    owners, _, _, cells = owned_ref.shape
    copies = [
        pltpu.make_async_copy(flat_ref.at[:, :, pl.ds(m * cells, cells)], owned_ref.at[m], sems.at[m])
        for m in range(owners)
    ]
    for copy in copies:
        copy.start()
    for copy in copies:
        copy.wait()


def homeward_kernel(owned_ref, flat_ref, sems):
    owners, _, _, cells = owned_ref.shape
    copies = [
        pltpu.make_async_copy(owned_ref.at[m], flat_ref.at[:, :, pl.ds(m * cells, cells)], sems.at[m])
        for m in range(owners)
    ]
    for copy in copies:
        copy.start()
    for copy in copies:
        copy.wait()


ANYWHERE = pl.BlockSpec(memory_space=pl.ANY)


def rearrange(kernel, array, shape, owners, name):
    return pl.pallas_call(
        kernel,
        out_shape=jax.ShapeDtypeStruct(shape, array.dtype),
        in_specs=[ANYWHERE],
        out_specs=ANYWHERE,
        scratch_shapes=[pltpu.SemaphoreType.DMA((owners,))],
        compiler_params=pltpu.CompilerParams(vmem_limit_bytes=2**17),
        name=name,
    )(array)


def fence_kernel(*refs):
    del refs


def fence(array, *before):
    return pl.pallas_call(
        fence_kernel,
        out_shape=jax.ShapeDtypeStruct(array.shape, array.dtype),
        in_specs=[ANYWHERE] * (1 + len(before)),
        out_specs=ANYWHERE,
        input_output_aliases={0: 0},
        compiler_params=pltpu.CompilerParams(vmem_limit_bytes=2**17),
        name="fence",
    )(array, *before)


def local(
    ensemble, obs_members, obs_value, obs_precision, tapering, routes, block_slots, block_counts
):
    mem_count = lax.axis_size("mem")
    fields, local_members, local_cells = ensemble.shape
    per_device = obs_members.shape[1] // mem_count
    owned_cells = local_cells // mem_count
    members = local_members * mem_count

    offset = lax.axis_index("mem") * per_device
    row_lists = routes[0, 0]
    targets, cap = row_lists.shape
    tiles = per_device // LANES
    both = jnp.concatenate(
        [
            lax.dynamic_slice_in_dim(obs_value, offset, per_device, 0).reshape(tiles, LANES),
            lax.dynamic_slice_in_dim(obs_precision, offset, per_device, 0).reshape(tiles, LANES),
        ],
        axis=0,
    )
    side = jnp.concatenate(
        [
            jnp.broadcast_to(both, (targets,) + both.shape),
            (row_lists >> 7).astype(BF16).reshape(targets, cap // LANES, LANES),
            (row_lists & (LANES - 1)).astype(BF16).reshape(targets, cap // LANES, LANES),
        ],
        axis=1,
    )
    me = lax.axis_index("pt")
    arrived = []
    for step in range(targets):
        mine = lax.dynamic_index_in_dim(side, me ^ step, 0, keepdims=False)
        arrived.append(lax.ppermute(mine, "pt", [(p, p ^ step) for p in range(targets)]) if step else mine)
    weight, value = spread_weights(
        me.reshape(1), block_slots[0, 0], tapering[0, 0], block_counts[0, 0], jnp.stack(arrived), tiles
    )

    split_obs = obs_members.reshape(local_members, mem_count, per_device)
    collected = lax.all_to_all(split_obs, "mem", split_axis=1, concat_axis=1, tiled=True)
    state = rearrange(
        outward_kernel, ensemble, (mem_count, fields, local_members, owned_cells), mem_count, "outward"
    )
    collected = fence(jnp.swapaxes(collected, 0, 1), state, side).reshape(members, per_device)
    pool = lax.all_gather(collected, "pt", axis=0, tiled=False)
    weights = solve_weights(pool, weight, value)

    state = lax.all_to_all(state, "mem", split_axis=0, concat_axis=0, tiled=True)
    analysed = apply_weights(state, weights)
    returned = lax.all_to_all(analysed, "mem", split_axis=0, concat_axis=0, tiled=True)
    return rearrange(homeward_kernel, returned, ensemble.shape, mem_count, "homeward")


def solution(mesh):
    placed = (
        P(None, "mem", "pt"),
        P("mem", "pt"),
        P("pt"),
        P("pt"),
        P("pt", "mem", None, None),
        P("mem", "pt", None, None),
        P("pt", "mem", None, None),
        P("pt", "mem", None),
    )
    return jax.shard_map(
        local, mesh=mesh, in_specs=placed, out_specs=P(None, "mem", "pt"), check_vma=False
    )
```

```python
import functools
import math

import jax
import jax.numpy as jnp
from jax import lax
from jax.experimental import pallas as pl
from jax.experimental.pallas import tpu as pltpu
from jax.sharding import PartitionSpec as P

NS_ITERS = 6
LANES = 128
CHUNK = 256
CAP_SHIFT = 3
CAP_ROWS = 1 << CAP_SHIFT
F32 = jnp.float32
BF16 = jnp.bfloat16
NN = (((1,), (0,)), ((), ()))
NT = (((1,), (1,)), ((), ()))
TN = (((0,), (0,)), ((), ()))


def scatter_kernel(me_ref, slots_ref, taper_ref, counts_ref, keep_ref, send_ref):
    blocks, width = slots_ref.shape
    rows = keep_ref.shape[1]
    cap_rows = CAP_ROWS
    core = me_ref[0] & 1
    position = lax.broadcasted_iota(jnp.int32, (1, width), 1)
    hi_iota = lax.broadcasted_iota(jnp.int32, (2 * rows, width), 0)
    lo_iota = lax.broadcasted_iota(jnp.int32, (LANES, width), 0)
    for b in range(blocks):
        slots = slots_ref[b : b + 1, :]
        live = position < counts_ref[b]
        value = jnp.where(live, taper_ref[b : b + 1, :].astype(F32), 0.0)
        slot_row = slots >> 7
        source = slot_row >> CAP_SHIFT
        place = ((source & 1) ^ core) * rows + (source >> 1) * cap_rows + (slot_row & (cap_rows - 1))
        hi = jnp.where(hi_iota == place, value, 0.0).astype(BF16)
        lo = jnp.where(lo_iota == (slots & (LANES - 1)), 1.0, 0.0).astype(BF16)
        spread = lax.dot_general(hi, lo, NT, preferred_element_type=F32)
        keep_ref[b] = spread[:rows]
        send_ref[b] = spread[rows:]


def scatter_taper(me, slots, taper, counts, sources):
    blocks = slots.shape[0]
    vmem = pl.BlockSpec(memory_space=pltpu.VMEM)
    smem = pl.BlockSpec(memory_space=pltpu.SMEM)
    half = jax.ShapeDtypeStruct((blocks, sources // 2 * CAP_ROWS, LANES), F32)
    return pl.pallas_call(
        scatter_kernel,
        out_shape=(half, half),
        in_specs=[smem, vmem, vmem, smem],
        out_specs=(vmem, vmem),
        compiler_params=pltpu.CompilerParams(vmem_limit_bytes=32 * 2**20),
        cost_estimate=pl.CostEstimate(flops=10**9, bytes_accessed=10**6, transcendentals=0),
        name="scatter_taper",
    )(me, slots, taper, counts)


def spread_kernel(me_ref, keep_ref, partner_ref, *refs):
    *side_refs, weight_ref, lhs_ref = refs
    blocks = keep_ref.shape[0]
    tiles = weight_ref.shape[2]
    parts = CAP_ROWS
    tile_iota = lax.broadcasted_iota(jnp.int32, (tiles, LANES), 0).astype(F32)
    lane_iota = lax.broadcasted_iota(jnp.int32, (LANES, LANES), 0).astype(F32)
    for step, side_ref in enumerate(side_refs):
        source = (me_ref[0] >> 1) ^ step
        precision = side_ref[tiles : 2 * tiles, :].astype(F32)
        for h, slot_ref in enumerate((keep_ref, partner_ref)):
            base = 2 * tiles + 2 * h * parts
            route_hi = side_ref[base : base + parts, :].astype(F32)
            route_lo = side_ref[base + parts : base + 2 * parts, :].astype(F32)
            onehots = []
            for c in range(parts):
                onehots.append(jnp.where(lane_iota == route_lo[c : c + 1, :], 1.0, 0.0).astype(BF16))
                in_tile = tile_iota == route_hi[c : c + 1, :]
                for b in range(blocks):
                    row = slot_ref[b, pl.ds(source * parts + c, 1), :]
                    lhs_ref[b * tiles : (b + 1) * tiles, c * LANES : (c + 1) * LANES] = jnp.where(
                        in_tile, row, 0.0
                    ).astype(BF16)
            rows = lax.dot_general(
                lhs_ref[...], jnp.concatenate(onehots, axis=1), NT, preferred_element_type=F32
            )
            for b in range(blocks):
                weight_ref[step, h * blocks + b] = rows[b * tiles : (b + 1) * tiles] * precision


def spread_weights(me, keep, partner, sides, tiles):
    blocks = keep.shape[0]
    vmem = pl.BlockSpec(memory_space=pltpu.VMEM)
    smem = pl.BlockSpec(memory_space=pltpu.SMEM)
    return pl.pallas_call(
        spread_kernel,
        out_shape=jax.ShapeDtypeStruct((len(sides), 2 * blocks, tiles, LANES), F32),
        in_specs=[smem, vmem, vmem] + [vmem] * len(sides),
        out_specs=vmem,
        scratch_shapes=[pltpu.VMEM((blocks * tiles, CAP_ROWS * LANES), BF16)],
        compiler_params=pltpu.CompilerParams(vmem_limit_bytes=32 * 2**20),
        cost_estimate=pl.CostEstimate(flops=10**9, bytes_accessed=10**6, transcendentals=0),
        name="spread_weights",
    )(me, keep, partner, *sides)


def halves_of(x):
    high = x.astype(BF16)
    return high, (x - high.astype(F32)).astype(BF16)


def product(a, b):
    a_high, a_low = halves_of(a)
    b_high, b_low = halves_of(b)
    return lax.dot_general(
        jnp.concatenate([a_high, a_high, a_low], axis=1),
        jnp.concatenate([b_high, b_low, b_high], axis=0),
        NN,
        preferred_element_type=F32,
    )


def gram_kernel(weight_ref, *refs):
    count = weight_ref.shape[0]
    piece_refs, side_refs = refs[:count], refs[count : 2 * count]
    own_ref, other_ref = refs[2 * count :]
    blocks = weight_ref.shape[1]
    owners, local_members, rows = piece_refs[0].shape
    members = owners * local_members
    half = blocks * members // 2
    extra_iota = lax.broadcasted_iota(jnp.int32, (LANES - members, LANES), 0)
    own_ref[...] = jnp.zeros_like(own_ref)
    other_ref[...] = jnp.zeros_like(other_ref)
    for s in range(count):
        piece_ref, side_ref = piece_refs[s], side_refs[s]
        values = side_ref[: rows // LANES, :].astype(F32)
        added = None
        for part in range(rows // CHUNK):
            lhs, rhs = [], []
            for u in range(CHUNK // LANES):
                t = part * (CHUNK // LANES) + u
                widened = piece_ref[:, :, t * LANES : (t + 1) * LANES].reshape(members, LANES).astype(F32)
                mean = jnp.sum(widened, axis=0, keepdims=True) / members
                perturbed = (widened - mean).astype(BF16)
                innovation = values[t : t + 1, :] - mean
                first = innovation.astype(BF16).astype(F32)
                rest = innovation - first
                second = rest.astype(BF16).astype(F32)
                third = rest - second
                innovations = jnp.where(
                    extra_iota == 0, first, jnp.where(extra_iota == 1, second, jnp.where(extra_iota == 2, third, 0.0))
                ).astype(BF16)
                rhs.append(jnp.concatenate([perturbed, innovations], axis=0))
                wide = perturbed.astype(F32)
                lhs.append(
                    jnp.concatenate(
                        [(wide * weight_ref[s, b, t : t + 1, :]).astype(BF16) for b in range(blocks)], axis=0
                    )
                )
            term = lax.dot_general(
                jnp.concatenate(lhs, axis=1), jnp.concatenate(rhs, axis=1), NT, preferred_element_type=F32
            )
            added = term if added is None else added + term
        own_ref[...] += added[:half]
        other_ref[...] += added[half:]


def gram_sums(weight, pieces, sides):
    blocks = weight.shape[1]
    owners, local_members, _ = pieces[0].shape
    vmem = pl.BlockSpec(memory_space=pltpu.VMEM)
    sums = jax.ShapeDtypeStruct((blocks // 2 * owners * local_members, LANES), F32)
    return pl.pallas_call(
        gram_kernel,
        out_shape=(sums, sums),
        in_specs=[vmem] * (1 + len(pieces) + len(sides)),
        out_specs=(vmem, vmem),
        compiler_params=pltpu.CompilerParams(vmem_limit_bytes=32 * 2**20),
        cost_estimate=pl.CostEstimate(flops=8 * 10**9, bytes_accessed=3 * 10**6, transcendentals=0),
        name="gram_sums",
    )(weight, *pieces, *sides)


def solve_kernel(own_ref, other_ref, out_ref):
    pairs, twice, _ = out_ref.shape
    members = twice // 2
    row = lax.broadcasted_iota(jnp.int32, (twice, twice), 0)
    column = lax.broadcasted_iota(jnp.int32, (twice, twice), 1)
    identity = jnp.where(row == column, 1.0, 0.0)
    same = (row < members) == (column < members)
    upper = lax.broadcasted_iota(jnp.int32, (twice, 1), 0) < members
    halves, scales, projections = [], [], []
    for p in range(pairs):
        total = own_ref[p * twice : (p + 1) * twice, :] + other_ref[p * twice : (p + 1) * twice, :]
        projections.append(jnp.sum(jnp.where(column < members, 0.0, total), axis=1, keepdims=True))
        shifted = pltpu.roll(total[members:], members, 1)
        gram = jnp.where(same, jnp.concatenate([total[:members], shifted], axis=0), 0.0)
        system = (members - 1.0) * identity + 0.5 * (gram + gram.T)
        squares = jnp.sum(system * system, axis=1, keepdims=True)
        frobenius = jnp.sqrt(
            jnp.where(
                upper,
                jnp.sum(jnp.where(upper, squares, 0.0), keepdims=True),
                jnp.sum(jnp.where(upper, 0.0, squares), keepdims=True),
            )
        )
        halves.append(system / frobenius)
        scales.append(jnp.sqrt(frobenius))
    inverses = []
    for sweep in range(NS_ITERS):
        updates = [
            1.5 * identity - 0.5 * (product(inverses[p], halves[p]) if sweep else halves[p]) for p in range(pairs)
        ]
        if sweep == 0:
            halves = [product(halves[p], updates[p]) for p in range(pairs)]
            inverses = updates
        elif sweep < NS_ITERS - 1:
            both = [product(jnp.concatenate([halves[p], inverses[p]], axis=0), updates[p]) for p in range(pairs)]
            halves = [x[:twice] for x in both]
            inverses = [x[twice:] for x in both]
        else:
            inverses = [product(inverses[p], updates[p]) for p in range(pairs)]
    for p in range(pairs):
        inverse_root = inverses[p] / scales[p]
        inner = jnp.sum(inverse_root * projections[p], axis=0, keepdims=True)
        mean_shift = jnp.sum(inverse_root * inner, axis=1, keepdims=True)
        out_ref[p] = jnp.where(same, math.sqrt(members - 1.0) * inverse_root + mean_shift, 0.0).astype(BF16)


def solve_weights(own, other, members):
    vmem = pl.BlockSpec(memory_space=pltpu.VMEM)
    twice = 2 * members
    return pl.pallas_call(
        solve_kernel,
        out_shape=jax.ShapeDtypeStruct((own.shape[0] // twice, twice, twice), BF16),
        in_specs=[vmem, vmem],
        out_specs=vmem,
        compiler_params=pltpu.CompilerParams(vmem_limit_bytes=32 * 2**20),
        cost_estimate=pl.CostEstimate(flops=3 * 10**9, bytes_accessed=10**6, transcendentals=0),
        name="solve_weights",
    )(own, other)


def apply_kernel(state_ref, weights_ref, out_ref):
    owners, fields, local_members, cells = state_ref.shape
    members = owners * local_members
    pairs, twice, _ = weights_ref.shape
    size = cells // (2 * pairs)
    for f in range(fields):
        for p in range(pairs):
            spans = [slice((2 * p + h) * size, (2 * p + h + 1) * size) for h in range(2)]
            means, deviations = [], []
            for span in spans:
                widened = state_ref[:, f, :, span].reshape(members, size).astype(F32)
                mean = jnp.sum(widened, axis=0, keepdims=True) / members
                means.append(mean)
                deviations.append((widened - mean).astype(BF16))
            moved = lax.dot_general(
                weights_ref[p], jnp.concatenate(deviations, axis=0), TN, preferred_element_type=F32
            )
            for h, span in enumerate(spans):
                out_ref[:, f, :, span] = (
                    (means[h] + moved[h * members : (h + 1) * members]).astype(BF16).reshape(owners, local_members, size)
                )


def apply_weights(state, weights):
    vmem = pl.BlockSpec(memory_space=pltpu.VMEM)
    return pl.pallas_call(
        apply_kernel,
        out_shape=jax.ShapeDtypeStruct(state.shape, BF16),
        in_specs=[vmem, vmem],
        out_specs=vmem,
        compiler_params=pltpu.CompilerParams(vmem_limit_bytes=32 * 2**20),
        cost_estimate=pl.CostEstimate(flops=10**9, bytes_accessed=2 * 10**6, transcendentals=0),
        name="apply_weights",
    )(state, weights)


def outward_kernel(flat_ref, owned_ref, sems):
    owners, _, _, cells = owned_ref.shape
    copies = [
        pltpu.make_async_copy(flat_ref.at[:, :, pl.ds(m * cells, cells)], owned_ref.at[m], sems.at[m])
        for m in range(owners)
    ]
    for copy in copies:
        copy.start()
    for copy in copies:
        copy.wait()


def homeward_kernel(owned_ref, flat_ref, sems):
    owners, _, _, cells = owned_ref.shape
    copies = [
        pltpu.make_async_copy(owned_ref.at[m], flat_ref.at[:, :, pl.ds(m * cells, cells)], sems.at[m])
        for m in range(owners)
    ]
    for copy in copies:
        copy.start()
    for copy in copies:
        copy.wait()


ANYWHERE = pl.BlockSpec(memory_space=pl.ANY)


def rearrange(kernel, array, shape, owners, name):
    return pl.pallas_call(
        kernel,
        out_shape=jax.ShapeDtypeStruct(shape, array.dtype),
        in_specs=[ANYWHERE],
        out_specs=ANYWHERE,
        scratch_shapes=[pltpu.SemaphoreType.DMA((owners,))],
        compiler_params=pltpu.CompilerParams(vmem_limit_bytes=2**17),
        name=name,
    )(array)


def fence_kernel(*refs):
    del refs


def fence(array, *before):
    return pl.pallas_call(
        fence_kernel,
        out_shape=jax.ShapeDtypeStruct(array.shape, array.dtype),
        in_specs=[ANYWHERE] * (1 + len(before)),
        out_specs=ANYWHERE,
        input_output_aliases={0: 0},
        compiler_params=pltpu.CompilerParams(vmem_limit_bytes=2**17),
        name="fence",
    )(array, *before)


def local(
    ensemble, obs_members, obs_value, obs_precision, tapering, routes, block_slots, block_counts
):
    mem_count = lax.axis_size("mem")
    fields, local_members, local_cells = ensemble.shape
    per_device = obs_members.shape[1] // mem_count
    owned_cells = local_cells // mem_count
    members = local_members * mem_count

    offset = lax.axis_index("mem") * per_device
    row_lists = routes[0, 0]
    targets, cap = row_lists.shape
    tiles = per_device // LANES
    both = jnp.concatenate(
        [
            lax.dynamic_slice_in_dim(obs_value, offset, per_device, 0).reshape(tiles, LANES),
            lax.dynamic_slice_in_dim(obs_precision, offset, per_device, 0).reshape(tiles, LANES),
        ],
        axis=0,
    )
    chips = targets // 2
    route_tiles = jnp.stack([row_lists >> 7, row_lists & (LANES - 1)], axis=1).astype(BF16)
    route_tiles = route_tiles.reshape(chips, 2, 2 * CAP_ROWS, LANES)
    me = lax.axis_index("pt")
    core = me & 1
    own_routes = lax.dynamic_index_in_dim(route_tiles, core, 1, keepdims=False)
    other_routes = lax.dynamic_index_in_dim(route_tiles, 1 - core, 1, keepdims=False)
    side = jnp.concatenate(
        [jnp.broadcast_to(both, (chips,) + both.shape), own_routes, other_routes], axis=1
    )

    def across(array, step):
        return lax.ppermute(array, "pt", [(p, p ^ step) for p in range(targets)])

    sides = []
    for step in range(chips):
        mine = lax.dynamic_index_in_dim(side, (me >> 1) ^ step, 0, keepdims=False)
        sides.append(across(mine, 2 * step) if step else mine)
    keep, send = scatter_taper(me.reshape(1), block_slots[0, 0], tapering[0, 0], block_counts[0, 0], targets)
    partner = across(send, 1)
    weight = spread_weights(me.reshape(1), keep, partner, sides, tiles)

    split_obs = obs_members.reshape(local_members, mem_count, per_device)
    collected = lax.all_to_all(split_obs, "mem", split_axis=1, concat_axis=1, tiled=True)
    state = rearrange(
        outward_kernel, ensemble, (mem_count, fields, local_members, owned_cells), mem_count, "outward"
    )
    state = fence(state, partner, *sides[1:])
    collected = fence(jnp.swapaxes(collected, 0, 1), state)
    pieces = [across(collected, 2 * step) if step else collected for step in range(chips)]
    own, other = gram_sums(weight, pieces, sides)
    weights = solve_weights(own, across(other, 1), members)

    state = lax.all_to_all(state, "mem", split_axis=0, concat_axis=0, tiled=True)
    analysed = apply_weights(state, weights)
    returned = lax.all_to_all(analysed, "mem", split_axis=0, concat_axis=0, tiled=True)
    return rearrange(homeward_kernel, returned, ensemble.shape, mem_count, "homeward")


def solution(mesh):
    placed = (
        P(None, "mem", "pt"),
        P("mem", "pt"),
        P("pt"),
        P("pt"),
        P("pt", "mem", None, None),
        P("mem", "pt", None, None),
        P("pt", "mem", None, None),
        P("pt", "mem", None),
    )
    return jax.shard_map(
        local, mesh=mesh, in_specs=placed, out_specs=P(None, "mem", "pt"), check_vma=False
    )
```

```python
import functools
import math

import jax
import jax.numpy as jnp
from jax import lax
from jax.experimental import pallas as pl
from jax.experimental.pallas import tpu as pltpu
from jax.sharding import PartitionSpec as P

NS_ITERS = 6
LANES = 128
CHUNK = 256
CAP_SHIFT = 3
CAP_ROWS = 1 << CAP_SHIFT
F32 = jnp.float32
BF16 = jnp.bfloat16
NN = (((1,), (0,)), ((), ()))
NT = (((1,), (1,)), ((), ()))
TN = (((0,), (0,)), ((), ()))


def scatter_kernel(me_ref, slots_ref, taper_ref, counts_ref, keep_ref, send_ref):
    blocks, width = slots_ref.shape
    rows = keep_ref.shape[1]
    cap_rows = CAP_ROWS
    core = me_ref[0] & 1
    position = lax.broadcasted_iota(jnp.int32, (1, width), 1)
    hi_iota = lax.broadcasted_iota(jnp.int32, (2 * rows, LANES), 0).astype(BF16)
    lo_iota = lax.broadcasted_iota(jnp.int32, (LANES, LANES), 0).astype(BF16)
    hi_iota = jnp.concatenate([hi_iota] * (width // LANES), axis=1)
    lo_iota = jnp.concatenate([lo_iota] * (width // LANES), axis=1)
    none, one = jnp.zeros((), BF16), jnp.ones((), BF16)
    for b in range(blocks):
        slots = slots_ref[b : b + 1, :]
        live = position < counts_ref[b]
        value = jnp.where(live, taper_ref[b : b + 1, :].astype(F32), 0.0).astype(BF16)
        slot_row = slots >> 7
        source = slot_row >> CAP_SHIFT
        place = ((source & 1) ^ core) * rows + (source >> 1) * cap_rows + (slot_row & (cap_rows - 1))
        hi = jnp.where(hi_iota == place.astype(F32).astype(BF16), value, none)
        lo = jnp.where(lo_iota == (slots & (LANES - 1)).astype(F32).astype(BF16), one, none)
        spread = lax.dot_general(hi, lo, NT, preferred_element_type=F32)
        keep_ref[b] = spread[:rows]
        send_ref[b] = spread[rows:]


def scatter_taper(me, slots, taper, counts, sources):
    blocks = slots.shape[0]
    vmem = pl.BlockSpec(memory_space=pltpu.VMEM)
    smem = pl.BlockSpec(memory_space=pltpu.SMEM)
    half = jax.ShapeDtypeStruct((blocks, sources // 2 * CAP_ROWS, LANES), F32)
    return pl.pallas_call(
        scatter_kernel,
        out_shape=(half, half),
        in_specs=[smem, vmem, vmem, smem],
        out_specs=(vmem, vmem),
        compiler_params=pltpu.CompilerParams(vmem_limit_bytes=32 * 2**20),
        cost_estimate=pl.CostEstimate(flops=10**9, bytes_accessed=10**6, transcendentals=0),
        name="scatter_taper",
    )(me, slots, taper, counts)


def spread_kernel(me_ref, keep_ref, partner_ref, *refs):
    *side_refs, weight_ref, lhs_ref = refs
    blocks = keep_ref.shape[0]
    tiles = weight_ref.shape[2]
    parts = CAP_ROWS
    tile_iota = lax.broadcasted_iota(jnp.int32, (tiles, LANES), 0).astype(F32)
    lane_iota = lax.broadcasted_iota(jnp.int32, (LANES, LANES), 0).astype(F32)
    for step, side_ref in enumerate(side_refs):
        source = (me_ref[0] >> 1) ^ step
        precision = side_ref[tiles : 2 * tiles, :].astype(F32)
        for h, slot_ref in enumerate((keep_ref, partner_ref)):
            base = 2 * tiles + 2 * h * parts
            route_hi = side_ref[base : base + parts, :].astype(F32)
            route_lo = side_ref[base + parts : base + 2 * parts, :].astype(F32)
            onehots = []
            for c in range(parts):
                onehots.append(jnp.where(lane_iota == route_lo[c : c + 1, :], 1.0, 0.0).astype(BF16))
                in_tile = tile_iota == route_hi[c : c + 1, :]
                for b in range(blocks):
                    row = slot_ref[b, pl.ds(source * parts + c, 1), :]
                    lhs_ref[b * tiles : (b + 1) * tiles, c * LANES : (c + 1) * LANES] = jnp.where(
                        in_tile, row, 0.0
                    ).astype(BF16)
            rows = lax.dot_general(
                lhs_ref[...], jnp.concatenate(onehots, axis=1), NT, preferred_element_type=F32
            )
            for b in range(blocks):
                weight_ref[step, h * blocks + b] = rows[b * tiles : (b + 1) * tiles] * precision


def spread_weights(me, keep, partner, sides, tiles):
    blocks = keep.shape[0]
    vmem = pl.BlockSpec(memory_space=pltpu.VMEM)
    smem = pl.BlockSpec(memory_space=pltpu.SMEM)
    return pl.pallas_call(
        spread_kernel,
        out_shape=jax.ShapeDtypeStruct((len(sides), 2 * blocks, tiles, LANES), F32),
        in_specs=[smem, vmem, vmem] + [vmem] * len(sides),
        out_specs=vmem,
        scratch_shapes=[pltpu.VMEM((blocks * tiles, CAP_ROWS * LANES), BF16)],
        compiler_params=pltpu.CompilerParams(vmem_limit_bytes=32 * 2**20),
        cost_estimate=pl.CostEstimate(flops=10**9, bytes_accessed=10**6, transcendentals=0),
        name="spread_weights",
    )(me, keep, partner, *sides)


def halves_of(x):
    high = x.astype(BF16)
    return high, (x - high.astype(F32)).astype(BF16)


def product(a, b):
    a_high, a_low = halves_of(a)
    b_high, b_low = halves_of(b)
    return lax.dot_general(
        jnp.concatenate([a_high, a_high, a_low], axis=1),
        jnp.concatenate([b_high, b_low, b_high], axis=0),
        NN,
        preferred_element_type=F32,
    )


def gram_kernel(first_piece, count, weight_ref, *refs):
    piece_refs, side_refs = refs[:count], refs[count : 2 * count]
    *before_refs, own_ref, other_ref = refs[2 * count :]
    blocks = weight_ref.shape[1]
    owners, local_members, rows = piece_refs[0].shape
    members = owners * local_members
    half = blocks * members // 2
    extra_iota = lax.broadcasted_iota(jnp.int32, (LANES - members, LANES), 0)
    for s in range(count):
        piece_ref, side_ref = piece_refs[s], side_refs[s]
        values = side_ref[: rows // LANES, :].astype(F32)
        added = None
        for part in range(rows // CHUNK):
            lhs, rhs = [], []
            for u in range(CHUNK // LANES):
                t = part * (CHUNK // LANES) + u
                widened = piece_ref[:, :, t * LANES : (t + 1) * LANES].reshape(members, LANES).astype(F32)
                mean = jnp.sum(widened, axis=0, keepdims=True) / members
                perturbed = (widened - mean).astype(BF16)
                innovation = values[t : t + 1, :] - mean
                first = innovation.astype(BF16).astype(F32)
                rest = innovation - first
                second = rest.astype(BF16).astype(F32)
                third = rest - second
                innovations = jnp.where(
                    extra_iota == 0, first, jnp.where(extra_iota == 1, second, jnp.where(extra_iota == 2, third, 0.0))
                ).astype(BF16)
                rhs.append(jnp.concatenate([perturbed, innovations], axis=0))
                wide = perturbed.astype(F32)
                lhs.append(
                    jnp.concatenate(
                        [(wide * weight_ref[first_piece + s, b, t : t + 1, :]).astype(BF16) for b in range(blocks)], axis=0
                    )
                )
            term = lax.dot_general(
                jnp.concatenate(lhs, axis=1), jnp.concatenate(rhs, axis=1), NT, preferred_element_type=F32
            )
            added = term if added is None else added + term
        for at, ref in enumerate((own_ref, other_ref)):
            term = added[at * half : (at + 1) * half]
            if s:
                ref[...] += term
            elif before_refs:
                ref[...] = before_refs[at][...] + term
            else:
                ref[...] = term


def gram_sums(weight, pieces, sides, first_piece, before=()):
    blocks = weight.shape[1]
    owners, local_members, _ = pieces[0].shape
    vmem = pl.BlockSpec(memory_space=pltpu.VMEM)
    sums = jax.ShapeDtypeStruct((blocks // 2 * owners * local_members, LANES), F32)
    return pl.pallas_call(
        functools.partial(gram_kernel, first_piece, len(pieces)),
        out_shape=(sums, sums),
        in_specs=[vmem] * (1 + len(pieces) + len(sides) + len(before)),
        out_specs=(vmem, vmem),
        compiler_params=pltpu.CompilerParams(vmem_limit_bytes=32 * 2**20),
        cost_estimate=pl.CostEstimate(flops=len(pieces) * 2 * 10**9, bytes_accessed=10**6, transcendentals=0),
        name="gram_sums",
    )(weight, *pieces, *sides, *before)


def solve_kernel(own_ref, other_ref, out_ref):
    pairs, twice, _ = out_ref.shape
    members = twice // 2
    row = lax.broadcasted_iota(jnp.int32, (twice, twice), 0)
    column = lax.broadcasted_iota(jnp.int32, (twice, twice), 1)
    identity = jnp.where(row == column, 1.0, 0.0)
    same = (row < members) == (column < members)
    upper = lax.broadcasted_iota(jnp.int32, (twice, 1), 0) < members
    halves, scales, projections = [], [], []
    for p in range(pairs):
        total = own_ref[p * twice : (p + 1) * twice, :] + other_ref[p * twice : (p + 1) * twice, :]
        projections.append(jnp.sum(jnp.where(column < members, 0.0, total), axis=1, keepdims=True))
        shifted = pltpu.roll(total[members:], members, 1)
        gram = jnp.where(same, jnp.concatenate([total[:members], shifted], axis=0), 0.0)
        system = (members - 1.0) * identity + 0.5 * (gram + gram.T)
        squares = jnp.sum(system * system, axis=1, keepdims=True)
        frobenius = jnp.sqrt(
            jnp.where(
                upper,
                jnp.sum(jnp.where(upper, squares, 0.0), keepdims=True),
                jnp.sum(jnp.where(upper, 0.0, squares), keepdims=True),
            )
        )
        halves.append(system / frobenius)
        scales.append(jnp.sqrt(frobenius))
    inverses = []
    for sweep in range(NS_ITERS):
        updates = [
            1.5 * identity - 0.5 * (product(inverses[p], halves[p]) if sweep else halves[p]) for p in range(pairs)
        ]
        if sweep == 0:
            halves = [product(halves[p], updates[p]) for p in range(pairs)]
            inverses = updates
        elif sweep < NS_ITERS - 1:
            both = [product(jnp.concatenate([halves[p], inverses[p]], axis=0), updates[p]) for p in range(pairs)]
            halves = [x[:twice] for x in both]
            inverses = [x[twice:] for x in both]
        else:
            inverses = [product(inverses[p], updates[p]) for p in range(pairs)]
    for p in range(pairs):
        inverse_root = inverses[p] / scales[p]
        inner = jnp.sum(inverse_root * projections[p], axis=0, keepdims=True)
        mean_shift = jnp.sum(inverse_root * inner, axis=1, keepdims=True)
        out_ref[p] = jnp.where(same, math.sqrt(members - 1.0) * inverse_root + mean_shift, 0.0).astype(BF16)


def solve_weights(own, other, members):
    vmem = pl.BlockSpec(memory_space=pltpu.VMEM)
    twice = 2 * members
    return pl.pallas_call(
        solve_kernel,
        out_shape=jax.ShapeDtypeStruct((own.shape[0] // twice, twice, twice), BF16),
        in_specs=[vmem, vmem],
        out_specs=vmem,
        compiler_params=pltpu.CompilerParams(vmem_limit_bytes=32 * 2**20),
        cost_estimate=pl.CostEstimate(flops=3 * 10**9, bytes_accessed=10**6, transcendentals=0),
        name="solve_weights",
    )(own, other)


def apply_kernel(state_ref, weights_ref, out_ref):
    owners, fields, local_members, cells = state_ref.shape
    members = owners * local_members
    pairs, twice, _ = weights_ref.shape
    size = cells // (2 * pairs)
    for f in range(fields):
        for p in range(pairs):
            spans = [slice((2 * p + h) * size, (2 * p + h + 1) * size) for h in range(2)]
            means, deviations = [], []
            for span in spans:
                widened = state_ref[:, f, :, span].reshape(members, size).astype(F32)
                mean = jnp.sum(widened, axis=0, keepdims=True) / members
                means.append(mean)
                deviations.append((widened - mean).astype(BF16))
            moved = lax.dot_general(
                weights_ref[p], jnp.concatenate(deviations, axis=0), TN, preferred_element_type=F32
            )
            for h, span in enumerate(spans):
                out_ref[:, f, :, span] = (
                    (means[h] + moved[h * members : (h + 1) * members]).astype(BF16).reshape(owners, local_members, size)
                )


def apply_weights(state, weights):
    vmem = pl.BlockSpec(memory_space=pltpu.VMEM)
    return pl.pallas_call(
        apply_kernel,
        out_shape=jax.ShapeDtypeStruct(state.shape, BF16),
        in_specs=[vmem, vmem],
        out_specs=vmem,
        compiler_params=pltpu.CompilerParams(vmem_limit_bytes=32 * 2**20),
        cost_estimate=pl.CostEstimate(flops=10**9, bytes_accessed=2 * 10**6, transcendentals=0),
        name="apply_weights",
    )(state, weights)


def outward_kernel(flat_ref, owned_ref, sems):
    owners, _, _, cells = owned_ref.shape
    copies = [
        pltpu.make_async_copy(flat_ref.at[:, :, pl.ds(m * cells, cells)], owned_ref.at[m], sems.at[m])
        for m in range(owners)
    ]
    for copy in copies:
        copy.start()
    for copy in copies:
        copy.wait()


def homeward_kernel(owned_ref, flat_ref, sems):
    owners, _, _, cells = owned_ref.shape
    copies = [
        pltpu.make_async_copy(owned_ref.at[m], flat_ref.at[:, :, pl.ds(m * cells, cells)], sems.at[m])
        for m in range(owners)
    ]
    for copy in copies:
        copy.start()
    for copy in copies:
        copy.wait()


ANYWHERE = pl.BlockSpec(memory_space=pl.ANY)


def rearrange(kernel, array, shape, owners, name):
    return pl.pallas_call(
        kernel,
        out_shape=jax.ShapeDtypeStruct(shape, array.dtype),
        in_specs=[ANYWHERE],
        out_specs=ANYWHERE,
        scratch_shapes=[pltpu.SemaphoreType.DMA((owners,))],
        compiler_params=pltpu.CompilerParams(vmem_limit_bytes=2**17),
        name=name,
    )(array)


def fence_kernel(*refs):
    del refs


def fence(array, *before):
    return pl.pallas_call(
        fence_kernel,
        out_shape=jax.ShapeDtypeStruct(array.shape, array.dtype),
        in_specs=[ANYWHERE] * (1 + len(before)),
        out_specs=ANYWHERE,
        input_output_aliases={0: 0},
        compiler_params=pltpu.CompilerParams(vmem_limit_bytes=2**17),
        name="fence",
    )(array, *before)


def local(
    ensemble, obs_members, obs_value, obs_precision, tapering, routes, block_slots, block_counts
):
    mem_count = lax.axis_size("mem")
    fields, local_members, local_cells = ensemble.shape
    per_device = obs_members.shape[1] // mem_count
    owned_cells = local_cells // mem_count
    members = local_members * mem_count

    offset = lax.axis_index("mem") * per_device
    row_lists = routes[0, 0]
    targets, cap = row_lists.shape
    tiles = per_device // LANES
    both = jnp.concatenate(
        [
            lax.dynamic_slice_in_dim(obs_value, offset, per_device, 0).reshape(tiles, LANES),
            lax.dynamic_slice_in_dim(obs_precision, offset, per_device, 0).reshape(tiles, LANES),
        ],
        axis=0,
    )
    chips = targets // 2
    route_tiles = jnp.stack([row_lists >> 7, row_lists & (LANES - 1)], axis=1).astype(BF16)
    route_tiles = route_tiles.reshape(chips, 2, 2 * CAP_ROWS, LANES)
    me = lax.axis_index("pt")
    core = me & 1
    own_routes = lax.dynamic_index_in_dim(route_tiles, core, 1, keepdims=False)
    other_routes = lax.dynamic_index_in_dim(route_tiles, 1 - core, 1, keepdims=False)
    side = jnp.concatenate(
        [jnp.broadcast_to(both, (chips,) + both.shape), own_routes, other_routes], axis=1
    )

    def across(array, step):
        return lax.ppermute(array, "pt", [(p, p ^ step) for p in range(targets)])

    sides = []
    for step in range(chips):
        mine = lax.dynamic_index_in_dim(side, (me >> 1) ^ step, 0, keepdims=False)
        sides.append(across(mine, 2 * step) if step else mine)
    keep, send = scatter_taper(me.reshape(1), block_slots[0, 0], tapering[0, 0], block_counts[0, 0], targets)
    partner = across(send, 1)
    weight = spread_weights(me.reshape(1), keep, partner, sides, tiles)

    split_obs = obs_members.reshape(local_members, mem_count, per_device)
    collected = lax.all_to_all(split_obs, "mem", split_axis=1, concat_axis=1, tiled=True)
    state = rearrange(
        outward_kernel, ensemble, (mem_count, fields, local_members, owned_cells), mem_count, "outward"
    )
    state = fence(state, send, *sides[1:])
    collected = fence(jnp.swapaxes(collected, 0, 1), state)
    pieces = [across(collected, 2 * step) if step else collected for step in range(chips)]
    begun = gram_sums(weight, pieces[:1], sides[:1], 0)
    own, other = gram_sums(weight, pieces[1:], sides[1:], 1, begun)
    weights = solve_weights(own, across(other, 1), members)

    state = lax.all_to_all(state, "mem", split_axis=0, concat_axis=0, tiled=True)
    analysed = apply_weights(state, weights)
    returned = lax.all_to_all(analysed, "mem", split_axis=0, concat_axis=0, tiled=True)
    return rearrange(homeward_kernel, returned, ensemble.shape, mem_count, "homeward")


def solution(mesh):
    placed = (
        P(None, "mem", "pt"),
        P("mem", "pt"),
        P("pt"),
        P("pt"),
        P("pt", "mem", None, None),
        P("mem", "pt", None, None),
        P("pt", "mem", None, None),
        P("pt", "mem", None),
    )
    return jax.shard_map(
        local, mesh=mesh, in_specs=placed, out_specs=P(None, "mem", "pt"), check_vma=False
    )
```

```python
import functools
import math

import jax
import jax.numpy as jnp
from jax import lax
from jax.experimental import pallas as pl
from jax.experimental.pallas import tpu as pltpu
from jax.sharding import PartitionSpec as P

NS_ITERS = 6
LANES = 128
CHUNK = 256
GROUP = 8
CAP_SHIFT = 3
CAP_ROWS = 1 << CAP_SHIFT
F32 = jnp.float32
BF16 = jnp.bfloat16
NN = (((1,), (0,)), ((), ()))
NT = (((1,), (1,)), ((), ()))
TN = (((0,), (0,)), ((), ()))


def scatter_kernel(me_ref, slots_ref, taper_ref, counts_ref, keep_ref, send_ref):
    blocks, width = slots_ref.shape
    rows = keep_ref.shape[1]
    cap_rows = CAP_ROWS
    core = me_ref[0] & 1
    position = lax.broadcasted_iota(jnp.int32, (1, width), 1)
    hi_iota = lax.broadcasted_iota(jnp.int32, (2 * rows, LANES), 0).astype(BF16)
    lo_iota = lax.broadcasted_iota(jnp.int32, (LANES, LANES), 0).astype(BF16)
    hi_iota = jnp.concatenate([hi_iota] * (width // LANES), axis=1)
    lo_iota = jnp.concatenate([lo_iota] * (width // LANES), axis=1)
    none, one = jnp.zeros((), BF16), jnp.ones((), BF16)
    for b in range(blocks):
        slots = slots_ref[b : b + 1, :]
        live = position < counts_ref[b]
        value = jnp.where(live, taper_ref[b : b + 1, :].astype(F32), 0.0).astype(BF16)
        slot_row = slots >> 7
        source = slot_row >> CAP_SHIFT
        place = ((source & 1) ^ core) * rows + (source >> 1) * cap_rows + (slot_row & (cap_rows - 1))
        hi = jnp.where(hi_iota == place.astype(F32).astype(BF16), value, none)
        lo = jnp.where(lo_iota == (slots & (LANES - 1)).astype(F32).astype(BF16), one, none)
        spread = lax.dot_general(hi, lo, NT, preferred_element_type=F32)
        keep_ref[b] = spread[:rows]
        send_ref[b] = spread[rows:]


def scatter_taper(me, slots, taper, counts, sources):
    blocks = slots.shape[0]
    vmem = pl.BlockSpec(memory_space=pltpu.VMEM)
    smem = pl.BlockSpec(memory_space=pltpu.SMEM)
    half = jax.ShapeDtypeStruct((blocks, sources // 2 * CAP_ROWS, LANES), F32)
    return pl.pallas_call(
        scatter_kernel,
        out_shape=(half, half),
        in_specs=[smem, vmem, vmem, smem],
        out_specs=(vmem, vmem),
        compiler_params=pltpu.CompilerParams(vmem_limit_bytes=32 * 2**20),
        cost_estimate=pl.CostEstimate(flops=10**9, bytes_accessed=10**6, transcendentals=0),
        name="scatter_taper",
    )(me, slots, taper, counts)


def spread_kernel(me_ref, keep_ref, partner_ref, *refs):
    *side_refs, weight_ref, lhs_ref = refs
    blocks = keep_ref.shape[0]
    tiles = weight_ref.shape[2]
    parts = CAP_ROWS
    tile_iota = lax.broadcasted_iota(jnp.int32, (tiles, LANES), 0).astype(F32)
    lane_iota = lax.broadcasted_iota(jnp.int32, (LANES, LANES), 0).astype(F32)
    for step, side_ref in enumerate(side_refs):
        source = (me_ref[0] >> 1) ^ step
        precision = side_ref[tiles : 2 * tiles, :].astype(F32)
        for h, slot_ref in enumerate((keep_ref, partner_ref)):
            base = 2 * tiles + 2 * h * parts
            route_hi = side_ref[base : base + parts, :].astype(F32)
            route_lo = side_ref[base + parts : base + 2 * parts, :].astype(F32)
            onehots = []
            for c in range(parts):
                onehots.append(jnp.where(lane_iota == route_lo[c : c + 1, :], 1.0, 0.0).astype(BF16))
                in_tile = tile_iota == route_hi[c : c + 1, :]
                for b in range(blocks):
                    row = slot_ref[b, pl.ds(source * parts + c, 1), :]
                    lhs_ref[b * tiles : (b + 1) * tiles, c * LANES : (c + 1) * LANES] = jnp.where(
                        in_tile, row, 0.0
                    ).astype(BF16)
            rows = lax.dot_general(
                lhs_ref[...], jnp.concatenate(onehots, axis=1), NT, preferred_element_type=F32
            )
            for b in range(blocks):
                weight_ref[step, h * blocks + b] = rows[b * tiles : (b + 1) * tiles] * precision


def spread_weights(me, keep, partner, sides, tiles):
    blocks = keep.shape[0]
    vmem = pl.BlockSpec(memory_space=pltpu.VMEM)
    smem = pl.BlockSpec(memory_space=pltpu.SMEM)
    return pl.pallas_call(
        spread_kernel,
        out_shape=jax.ShapeDtypeStruct((len(sides), 2 * blocks, tiles, LANES), F32),
        in_specs=[smem, vmem, vmem] + [vmem] * len(sides),
        out_specs=vmem,
        scratch_shapes=[pltpu.VMEM((blocks * tiles, CAP_ROWS * LANES), BF16)],
        compiler_params=pltpu.CompilerParams(vmem_limit_bytes=32 * 2**20),
        cost_estimate=pl.CostEstimate(flops=10**9, bytes_accessed=10**6, transcendentals=0),
        name="spread_weights",
    )(me, keep, partner, *sides)


def member_rows(ref, at, span):
    owners, local_members = ref.shape[0], ref.shape[-2]
    width = span.stop - span.start
    return jnp.concatenate(
        [
            ref[(slice(g, g + GROUP), *at, slice(None), span)].reshape(GROUP * local_members, width)
            for g in range(0, owners, GROUP)
        ],
        axis=0,
    )


def halves_of(x):
    high = x.astype(BF16)
    return high, (x - high.astype(F32)).astype(BF16)


def product(a, b):
    a_high, a_low = halves_of(a)
    b_high, b_low = halves_of(b)
    return lax.dot_general(
        jnp.concatenate([a_high, a_high, a_low], axis=1),
        jnp.concatenate([b_high, b_low, b_high], axis=0),
        NN,
        preferred_element_type=F32,
    )


def gram_kernel(first_piece, count, weight_ref, *refs):
    piece_refs, side_refs = refs[:count], refs[count : 2 * count]
    *before_refs, own_ref, other_ref = refs[2 * count :]
    blocks = weight_ref.shape[1]
    owners, local_members, rows = piece_refs[0].shape
    members = owners * local_members
    half = blocks * members // 2
    extra_iota = lax.broadcasted_iota(jnp.int32, (LANES - members, LANES), 0)
    for s in range(count):
        piece_ref, side_ref = piece_refs[s], side_refs[s]
        values = side_ref[: rows // LANES, :].astype(F32)
        added = None
        for part in range(rows // CHUNK):
            lhs, rhs = [], []
            for u in range(CHUNK // LANES):
                t = part * (CHUNK // LANES) + u
                widened = member_rows(piece_ref, (), slice(t * LANES, (t + 1) * LANES)).astype(F32)
                mean = jnp.sum(widened, axis=0, keepdims=True) / members
                perturbed = (widened - mean).astype(BF16)
                innovation = values[t : t + 1, :] - mean
                first = innovation.astype(BF16).astype(F32)
                rest = innovation - first
                second = rest.astype(BF16).astype(F32)
                third = rest - second
                innovations = jnp.where(
                    extra_iota == 0, first, jnp.where(extra_iota == 1, second, jnp.where(extra_iota == 2, third, 0.0))
                ).astype(BF16)
                rhs.append(jnp.concatenate([perturbed, innovations], axis=0))
                wide = perturbed.astype(F32)
                lhs.append(
                    jnp.concatenate(
                        [(wide * weight_ref[first_piece + s, b, t : t + 1, :]).astype(BF16) for b in range(blocks)], axis=0
                    )
                )
            term = lax.dot_general(
                jnp.concatenate(lhs, axis=1), jnp.concatenate(rhs, axis=1), NT, preferred_element_type=F32
            )
            added = term if added is None else added + term
        for at, ref in enumerate((own_ref, other_ref)):
            term = added[at * half : (at + 1) * half]
            if s:
                ref[...] += term
            elif before_refs:
                ref[...] = before_refs[at][...] + term
            else:
                ref[...] = term


def gram_sums(weight, pieces, sides, first_piece, before=()):
    blocks = weight.shape[1]
    owners, local_members, _ = pieces[0].shape
    vmem = pl.BlockSpec(memory_space=pltpu.VMEM)
    sums = jax.ShapeDtypeStruct((blocks // 2 * owners * local_members, LANES), F32)
    return pl.pallas_call(
        functools.partial(gram_kernel, first_piece, len(pieces)),
        out_shape=(sums, sums),
        in_specs=[vmem] * (1 + len(pieces) + len(sides) + len(before)),
        out_specs=(vmem, vmem),
        compiler_params=pltpu.CompilerParams(vmem_limit_bytes=32 * 2**20),
        cost_estimate=pl.CostEstimate(flops=len(pieces) * 2 * 10**9, bytes_accessed=10**6, transcendentals=0),
        name="gram_sums",
    )(weight, *pieces, *sides, *before)


def solve_kernel(own_ref, other_ref, out_ref):
    pairs, twice, _ = out_ref.shape
    members = twice // 2
    row = lax.broadcasted_iota(jnp.int32, (twice, twice), 0)
    column = lax.broadcasted_iota(jnp.int32, (twice, twice), 1)
    identity = jnp.where(row == column, 1.0, 0.0)
    same = (row < members) == (column < members)
    upper = lax.broadcasted_iota(jnp.int32, (twice, 1), 0) < members
    halves, scales, projections = [], [], []
    for p in range(pairs):
        total = own_ref[p * twice : (p + 1) * twice, :] + other_ref[p * twice : (p + 1) * twice, :]
        projections.append(jnp.sum(jnp.where(column < members, 0.0, total), axis=1, keepdims=True))
        shifted = pltpu.roll(total[members:], members, 1)
        gram = jnp.where(same, jnp.concatenate([total[:members], shifted], axis=0), 0.0)
        system = (members - 1.0) * identity + 0.5 * (gram + gram.T)
        squares = jnp.sum(system * system, axis=1, keepdims=True)
        frobenius = jnp.sqrt(
            jnp.where(
                upper,
                jnp.sum(jnp.where(upper, squares, 0.0), keepdims=True),
                jnp.sum(jnp.where(upper, 0.0, squares), keepdims=True),
            )
        )
        halves.append(system / frobenius)
        scales.append(jnp.sqrt(frobenius))
    inverses = []
    for sweep in range(NS_ITERS):
        updates = [
            1.5 * identity - 0.5 * (product(inverses[p], halves[p]) if sweep else halves[p]) for p in range(pairs)
        ]
        if sweep == 0:
            halves = [product(halves[p], updates[p]) for p in range(pairs)]
            inverses = updates
        elif sweep < NS_ITERS - 1:
            both = [product(jnp.concatenate([halves[p], inverses[p]], axis=0), updates[p]) for p in range(pairs)]
            halves = [x[:twice] for x in both]
            inverses = [x[twice:] for x in both]
        else:
            inverses = [product(inverses[p], updates[p]) for p in range(pairs)]
    for p in range(pairs):
        inverse_root = inverses[p] / scales[p]
        inner = jnp.sum(inverse_root * projections[p], axis=0, keepdims=True)
        mean_shift = jnp.sum(inverse_root * inner, axis=1, keepdims=True)
        out_ref[p] = jnp.where(same, math.sqrt(members - 1.0) * inverse_root + mean_shift, 0.0).astype(BF16)


def solve_weights(own, other, members):
    vmem = pl.BlockSpec(memory_space=pltpu.VMEM)
    twice = 2 * members
    return pl.pallas_call(
        solve_kernel,
        out_shape=jax.ShapeDtypeStruct((own.shape[0] // twice, twice, twice), BF16),
        in_specs=[vmem, vmem],
        out_specs=vmem,
        compiler_params=pltpu.CompilerParams(vmem_limit_bytes=32 * 2**20),
        cost_estimate=pl.CostEstimate(flops=3 * 10**9, bytes_accessed=10**6, transcendentals=0),
        name="solve_weights",
    )(own, other)


def apply_kernel(state_ref, weights_ref, out_ref):
    owners, fields, local_members, cells = state_ref.shape
    members = owners * local_members
    pairs, twice, _ = weights_ref.shape
    size = cells // (2 * pairs)
    for f in range(fields):
        for p in range(pairs):
            spans = [slice((2 * p + h) * size, (2 * p + h + 1) * size) for h in range(2)]
            means, deviations = [], []
            for span in spans:
                widened = member_rows(state_ref, (f,), span).astype(F32)
                mean = jnp.sum(widened, axis=0, keepdims=True) / members
                means.append(mean)
                deviations.append((widened - mean).astype(BF16))
            moved = lax.dot_general(
                weights_ref[p], jnp.concatenate(deviations, axis=0), TN, preferred_element_type=F32
            )
            for h, span in enumerate(spans):
                out_ref[:, f, :, span] = (
                    (means[h] + moved[h * members : (h + 1) * members]).astype(BF16).reshape(owners, local_members, size)
                )


def apply_weights(state, weights):
    vmem = pl.BlockSpec(memory_space=pltpu.VMEM)
    return pl.pallas_call(
        apply_kernel,
        out_shape=jax.ShapeDtypeStruct(state.shape, BF16),
        in_specs=[vmem, vmem],
        out_specs=vmem,
        compiler_params=pltpu.CompilerParams(vmem_limit_bytes=32 * 2**20),
        cost_estimate=pl.CostEstimate(flops=10**9, bytes_accessed=2 * 10**6, transcendentals=0),
        name="apply_weights",
    )(state, weights)


ANYWHERE = pl.BlockSpec(memory_space=pl.ANY)


def swap_kernel(from_ref, to_ref, sems):
    copies = [
        pltpu.make_async_copy(from_ref.at[:, k], to_ref.at[k], sems.at[k])
        if from_ref.shape[0] > from_ref.shape[1]
        else pltpu.make_async_copy(from_ref.at[k], to_ref.at[:, k], sems.at[k])
        for k in range(sems.shape[0])
    ]
    for copy in copies:
        copy.start()
    for copy in copies:
        copy.wait()


def swap_leading(array, name):
    first, second, *rest = array.shape
    return pl.pallas_call(
        swap_kernel,
        out_shape=jax.ShapeDtypeStruct((second, first, *rest), array.dtype),
        in_specs=[ANYWHERE],
        out_specs=ANYWHERE,
        scratch_shapes=[pltpu.SemaphoreType.DMA((min(first, second),))],
        compiler_params=pltpu.CompilerParams(vmem_limit_bytes=2**17),
        name=name,
    )(array)


def fence_kernel(*refs):
    del refs


def fence(array, *before):
    return pl.pallas_call(
        fence_kernel,
        out_shape=jax.ShapeDtypeStruct(array.shape, array.dtype),
        in_specs=[ANYWHERE] * (1 + len(before)),
        out_specs=ANYWHERE,
        input_output_aliases={0: 0},
        compiler_params=pltpu.CompilerParams(vmem_limit_bytes=2**17),
        name="fence",
    )(array, *before)


def local(
    ensemble, obs_members, obs_value, obs_precision, tapering, routes, block_slots, block_counts
):
    mem_count = lax.axis_size("mem")
    fields, local_members, local_cells = ensemble.shape
    per_device = obs_members.shape[1] // mem_count
    owned_cells = local_cells // mem_count
    members = local_members * mem_count

    offset = lax.axis_index("mem") * per_device
    row_lists = routes[0, 0]
    targets, cap = row_lists.shape
    tiles = per_device // LANES
    both = jnp.concatenate(
        [
            lax.dynamic_slice_in_dim(obs_value, offset, per_device, 0).reshape(tiles, LANES),
            lax.dynamic_slice_in_dim(obs_precision, offset, per_device, 0).reshape(tiles, LANES),
        ],
        axis=0,
    )
    chips = targets // 2
    route_tiles = jnp.stack([row_lists >> 7, row_lists & (LANES - 1)], axis=1).astype(BF16)
    route_tiles = route_tiles.reshape(chips, 2, 2 * CAP_ROWS, LANES)
    me = lax.axis_index("pt")
    core = me & 1
    own_routes = lax.dynamic_index_in_dim(route_tiles, core, 1, keepdims=False)
    other_routes = lax.dynamic_index_in_dim(route_tiles, 1 - core, 1, keepdims=False)
    side = jnp.concatenate(
        [jnp.broadcast_to(both, (chips,) + both.shape), own_routes, other_routes], axis=1
    )

    def across(array, step):
        return lax.ppermute(array, "pt", [(p, p ^ step) for p in range(targets)])

    sides = []
    for step in range(chips):
        mine = lax.dynamic_index_in_dim(side, (me >> 1) ^ step, 0, keepdims=False)
        sides.append(across(mine, 2 * step) if step else mine)
    keep, send = scatter_taper(me.reshape(1), block_slots[0, 0], tapering[0, 0], block_counts[0, 0], targets)
    partner = across(send, 1)
    weight = spread_weights(me.reshape(1), keep, partner, sides, tiles)

    split_obs = obs_members.reshape(local_members, mem_count, per_device)
    collected = lax.all_to_all(split_obs, "mem", split_axis=1, concat_axis=1, tiled=True)
    state = ensemble.reshape(fields, local_members, mem_count, owned_cells)
    state = swap_leading(jnp.swapaxes(state, 1, 2), "outward")
    state = fence(state, partner, *sides[1:])
    collected = fence(jnp.swapaxes(collected, 0, 1), state)
    pieces = [across(collected, 2 * step) if step else collected for step in range(chips)]
    begun = gram_sums(weight, pieces[:1], sides[:1], 0)
    own, other = gram_sums(weight, pieces[1:], sides[1:], 1, begun)
    weights = solve_weights(own, across(other, 1), members)

    state = lax.all_to_all(state, "mem", split_axis=0, concat_axis=0, tiled=True)
    analysed = apply_weights(state, weights)
    returned = lax.all_to_all(analysed, "mem", split_axis=0, concat_axis=0, tiled=True)
    returned = swap_leading(returned, "homeward")
    return jnp.swapaxes(returned, 1, 2).reshape(ensemble.shape)


def solution(mesh):
    placed = (
        P(None, "mem", "pt"),
        P("mem", "pt"),
        P("pt"),
        P("pt"),
        P("pt", "mem", None, None),
        P("mem", "pt", None, None),
        P("pt", "mem", None, None),
        P("pt", "mem", None),
    )
    return jax.shard_map(
        local, mesh=mesh, in_specs=placed, out_specs=P(None, "mem", "pt"), check_vma=False
    )
```

```python
import functools
import math

import jax
import jax.numpy as jnp
from jax import lax
from jax.experimental import pallas as pl
from jax.experimental.pallas import tpu as pltpu
from jax.sharding import PartitionSpec as P

NS_ITERS = 6
LANES = 128
CHUNK = 256
GROUP = 8
CAP_SHIFT = 3
CAP_ROWS = 1 << CAP_SHIFT
F32 = jnp.float32
BF16 = jnp.bfloat16
NN = (((1,), (0,)), ((), ()))
NT = (((1,), (1,)), ((), ()))
TN = (((0,), (0,)), ((), ()))


def scatter_kernel(me_ref, slots_ref, taper_ref, counts_ref, keep_ref, send_ref):
    blocks, width = slots_ref.shape
    rows = keep_ref.shape[1]
    cap_rows = CAP_ROWS
    core = me_ref[0] & 1
    position = lax.broadcasted_iota(jnp.int32, (1, width), 1)
    hi_iota = lax.broadcasted_iota(jnp.int32, (2 * rows, LANES), 0).astype(BF16)
    lo_iota = lax.broadcasted_iota(jnp.int32, (LANES, LANES), 0).astype(BF16)
    hi_iota = jnp.concatenate([hi_iota] * (width // LANES), axis=1)
    lo_iota = jnp.concatenate([lo_iota] * (width // LANES), axis=1)
    none, one = jnp.zeros((), BF16), jnp.ones((), BF16)
    taper = taper_ref[...].astype(F32)
    for b in range(blocks):
        slots = slots_ref[b : b + 1, :]
        live = position < counts_ref[b]
        value = jnp.where(live, taper[b : b + 1, :], 0.0).astype(BF16)
        slot_row = slots >> 7
        source = slot_row >> CAP_SHIFT
        place = ((source & 1) ^ core) * rows + (source >> 1) * cap_rows + (slot_row & (cap_rows - 1))
        hi = jnp.where(hi_iota == place.astype(F32).astype(BF16), value, none)
        lo = jnp.where(lo_iota == (slots & (LANES - 1)).astype(F32).astype(BF16), one, none)
        spread = lax.dot_general(hi, lo, NT, preferred_element_type=F32)
        keep_ref[b] = spread[:rows]
        send_ref[b] = spread[rows:]


def scatter_taper(me, slots, taper, counts, sources):
    blocks = slots.shape[0]
    vmem = pl.BlockSpec(memory_space=pltpu.VMEM)
    smem = pl.BlockSpec(memory_space=pltpu.SMEM)
    half = jax.ShapeDtypeStruct((blocks, sources // 2 * CAP_ROWS, LANES), F32)
    return pl.pallas_call(
        scatter_kernel,
        out_shape=(half, half),
        in_specs=[smem, vmem, vmem, smem],
        out_specs=(vmem, vmem),
        compiler_params=pltpu.CompilerParams(vmem_limit_bytes=32 * 2**20),
        cost_estimate=pl.CostEstimate(flops=10**9, bytes_accessed=10**6, transcendentals=0),
        name="scatter_taper",
    )(me, slots, taper, counts)


def spread_kernel(me_ref, keep_ref, partner_ref, *refs):
    *side_refs, weight_ref, lhs_ref = refs
    blocks = keep_ref.shape[0]
    tiles = weight_ref.shape[2]
    parts = CAP_ROWS
    tile_iota = lax.broadcasted_iota(jnp.int32, (tiles, LANES), 0).astype(F32)
    lane_iota = lax.broadcasted_iota(jnp.int32, (LANES, LANES), 0).astype(F32)
    for step, side_ref in enumerate(side_refs):
        source = (me_ref[0] >> 1) ^ step
        precision = side_ref[tiles : 2 * tiles, :].astype(F32)
        for h, slot_ref in enumerate((keep_ref, partner_ref)):
            base = 2 * tiles + 2 * h * parts
            route = side_ref[base : base + 2 * parts, :].astype(F32)
            route_hi, route_lo = route[:parts], route[parts:]
            onehots = []
            for c in range(parts):
                onehots.append(jnp.where(lane_iota == route_lo[c : c + 1, :], 1.0, 0.0).astype(BF16))
                in_tile = tile_iota == route_hi[c : c + 1, :]
                for b in range(blocks):
                    row = slot_ref[b, pl.ds(source * parts + c, 1), :]
                    lhs_ref[b * tiles : (b + 1) * tiles, c * LANES : (c + 1) * LANES] = jnp.where(
                        in_tile, row, 0.0
                    ).astype(BF16)
            rows = lax.dot_general(
                lhs_ref[...], jnp.concatenate(onehots, axis=1), NT, preferred_element_type=F32
            )
            for b in range(blocks):
                weight_ref[step, h * blocks + b] = rows[b * tiles : (b + 1) * tiles] * precision


def spread_weights(me, keep, partner, sides, tiles):
    blocks = keep.shape[0]
    vmem = pl.BlockSpec(memory_space=pltpu.VMEM)
    smem = pl.BlockSpec(memory_space=pltpu.SMEM)
    return pl.pallas_call(
        spread_kernel,
        out_shape=jax.ShapeDtypeStruct((len(sides), 2 * blocks, tiles, LANES), F32),
        in_specs=[smem, vmem, vmem] + [vmem] * len(sides),
        out_specs=vmem,
        scratch_shapes=[pltpu.VMEM((blocks * tiles, CAP_ROWS * LANES), BF16)],
        compiler_params=pltpu.CompilerParams(vmem_limit_bytes=32 * 2**20),
        cost_estimate=pl.CostEstimate(flops=10**9, bytes_accessed=10**6, transcendentals=0),
        name="spread_weights",
    )(me, keep, partner, *sides)


def member_rows(ref, at, span):
    owners, local_members = ref.shape[0], ref.shape[-2]
    width = span.stop - span.start
    return jnp.concatenate(
        [
            ref[(slice(g, g + GROUP), *at, slice(None), span)].reshape(GROUP * local_members, width)
            for g in range(0, owners, GROUP)
        ],
        axis=0,
    )


def halves_of(x):
    high = x.astype(BF16)
    return high, (x - high.astype(F32)).astype(BF16)


def product(a, b):
    a_high, a_low = halves_of(a)
    b_high, b_low = halves_of(b)
    return lax.dot_general(
        jnp.concatenate([a_high, a_high, a_low], axis=1),
        jnp.concatenate([b_high, b_low, b_high], axis=0),
        NN,
        preferred_element_type=F32,
    )


def gram_kernel(first_piece, count, weight_ref, *refs):
    piece_refs, side_refs = refs[:count], refs[count : 2 * count]
    *before_refs, own_ref, other_ref = refs[2 * count :]
    blocks = weight_ref.shape[1]
    owners, local_members, rows = piece_refs[0].shape
    members = owners * local_members
    half = blocks * members // 2
    extra_iota = lax.broadcasted_iota(jnp.int32, (LANES - members, LANES), 0)
    for s in range(count):
        piece_ref, side_ref = piece_refs[s], side_refs[s]
        values = side_ref[: rows // LANES, :].astype(F32)
        added = None
        for part in range(rows // CHUNK):
            lhs, rhs = [], []
            for u in range(CHUNK // LANES):
                t = part * (CHUNK // LANES) + u
                widened = member_rows(piece_ref, (), slice(t * LANES, (t + 1) * LANES)).astype(F32)
                mean = jnp.sum(widened, axis=0, keepdims=True) / members
                perturbed = (widened - mean).astype(BF16)
                innovation = values[t : t + 1, :] - mean
                first = innovation.astype(BF16).astype(F32)
                rest = innovation - first
                second = rest.astype(BF16).astype(F32)
                third = rest - second
                innovations = jnp.where(
                    extra_iota == 0, first, jnp.where(extra_iota == 1, second, jnp.where(extra_iota == 2, third, 0.0))
                ).astype(BF16)
                rhs.append(jnp.concatenate([perturbed, innovations], axis=0))
                wide = perturbed.astype(F32)
                lhs.append(
                    jnp.concatenate(
                        [(wide * weight_ref[first_piece + s, b, t : t + 1, :]).astype(BF16) for b in range(blocks)], axis=0
                    )
                )
            term = lax.dot_general(
                jnp.concatenate(lhs, axis=1), jnp.concatenate(rhs, axis=1), NT, preferred_element_type=F32
            )
            added = term if added is None else added + term
        for at, ref in enumerate((own_ref, other_ref)):
            term = added[at * half : (at + 1) * half]
            if s:
                ref[...] += term
            elif before_refs:
                ref[...] = before_refs[at][...] + term
            else:
                ref[...] = term


def gram_sums(weight, pieces, sides, first_piece, before=()):
    blocks = weight.shape[1]
    owners, local_members, _ = pieces[0].shape
    vmem = pl.BlockSpec(memory_space=pltpu.VMEM)
    sums = jax.ShapeDtypeStruct((blocks // 2 * owners * local_members, LANES), F32)
    return pl.pallas_call(
        functools.partial(gram_kernel, first_piece, len(pieces)),
        out_shape=(sums, sums),
        in_specs=[vmem] * (1 + len(pieces) + len(sides) + len(before)),
        out_specs=(vmem, vmem),
        compiler_params=pltpu.CompilerParams(vmem_limit_bytes=32 * 2**20),
        cost_estimate=pl.CostEstimate(flops=len(pieces) * 2 * 10**9, bytes_accessed=10**6, transcendentals=0),
        name="gram_sums",
    )(weight, *pieces, *sides, *before)


def solve_kernel(own_ref, other_ref, out_ref):
    pairs, twice, _ = out_ref.shape
    members = twice // 2
    row = lax.broadcasted_iota(jnp.int32, (twice, twice), 0)
    column = lax.broadcasted_iota(jnp.int32, (twice, twice), 1)
    identity = jnp.where(row == column, 1.0, 0.0)
    same = (row < members) == (column < members)
    upper = lax.broadcasted_iota(jnp.int32, (twice, 1), 0) < members
    halves, scales, projections = [], [], []
    for p in range(pairs):
        total = own_ref[p * twice : (p + 1) * twice, :] + other_ref[p * twice : (p + 1) * twice, :]
        projections.append(jnp.sum(jnp.where(column < members, 0.0, total), axis=1, keepdims=True))
        shifted = pltpu.roll(total[members:], members, 1)
        gram = jnp.where(same, jnp.concatenate([total[:members], shifted], axis=0), 0.0)
        system = (members - 1.0) * identity + 0.5 * (gram + gram.T)
        squares = jnp.sum(system * system, axis=1, keepdims=True)
        frobenius = jnp.sqrt(
            jnp.where(
                upper,
                jnp.sum(jnp.where(upper, squares, 0.0), keepdims=True),
                jnp.sum(jnp.where(upper, 0.0, squares), keepdims=True),
            )
        )
        halves.append(system / frobenius)
        scales.append(jnp.sqrt(frobenius))
    inverses = []
    for sweep in range(NS_ITERS):
        updates = [
            1.5 * identity - 0.5 * (product(inverses[p], halves[p]) if sweep else halves[p]) for p in range(pairs)
        ]
        if sweep == 0:
            halves = [product(halves[p], updates[p]) for p in range(pairs)]
            inverses = updates
        elif sweep < NS_ITERS - 1:
            both = [product(jnp.concatenate([halves[p], inverses[p]], axis=0), updates[p]) for p in range(pairs)]
            halves = [x[:twice] for x in both]
            inverses = [x[twice:] for x in both]
        else:
            inverses = [product(inverses[p], updates[p]) for p in range(pairs)]
    for p in range(pairs):
        inverse_root = inverses[p] / scales[p]
        inner = jnp.sum(inverse_root * projections[p], axis=0, keepdims=True)
        mean_shift = jnp.sum(inverse_root * inner, axis=1, keepdims=True)
        out_ref[p] = jnp.where(same, math.sqrt(members - 1.0) * inverse_root + mean_shift, 0.0).astype(BF16)


def solve_weights(own, other, members):
    vmem = pl.BlockSpec(memory_space=pltpu.VMEM)
    twice = 2 * members
    return pl.pallas_call(
        solve_kernel,
        out_shape=jax.ShapeDtypeStruct((own.shape[0] // twice, twice, twice), BF16),
        in_specs=[vmem, vmem],
        out_specs=vmem,
        compiler_params=pltpu.CompilerParams(vmem_limit_bytes=32 * 2**20),
        cost_estimate=pl.CostEstimate(flops=3 * 10**9, bytes_accessed=10**6, transcendentals=0),
        name="solve_weights",
    )(own, other)


def apply_kernel(state_ref, weights_ref, out_ref):
    owners, fields, local_members, cells = state_ref.shape
    members = owners * local_members
    pairs, twice, _ = weights_ref.shape
    size = cells // (2 * pairs)
    for f in range(fields):
        for p in range(pairs):
            spans = [slice((2 * p + h) * size, (2 * p + h + 1) * size) for h in range(2)]
            means, deviations = [], []
            for span in spans:
                widened = member_rows(state_ref, (f,), span).astype(F32)
                mean = jnp.sum(widened, axis=0, keepdims=True) / members
                means.append(mean)
                deviations.append((widened - mean).astype(BF16))
            moved = lax.dot_general(
                weights_ref[p], jnp.concatenate(deviations, axis=0), TN, preferred_element_type=F32
            )
            for h, span in enumerate(spans):
                out_ref[:, f, :, span] = (
                    (means[h] + moved[h * members : (h + 1) * members]).astype(BF16).reshape(owners, local_members, size)
                )


def apply_weights(state, weights):
    vmem = pl.BlockSpec(memory_space=pltpu.VMEM)
    return pl.pallas_call(
        apply_kernel,
        out_shape=jax.ShapeDtypeStruct(state.shape, BF16),
        in_specs=[vmem, vmem],
        out_specs=vmem,
        compiler_params=pltpu.CompilerParams(vmem_limit_bytes=32 * 2**20),
        cost_estimate=pl.CostEstimate(flops=10**9, bytes_accessed=2 * 10**6, transcendentals=0),
        name="apply_weights",
    )(state, weights)


ANYWHERE = pl.BlockSpec(memory_space=pl.ANY)


def swap_kernel(from_ref, to_ref, sems):
    copies = [
        pltpu.make_async_copy(from_ref.at[:, k], to_ref.at[k], sems.at[k])
        if from_ref.shape[0] > from_ref.shape[1]
        else pltpu.make_async_copy(from_ref.at[k], to_ref.at[:, k], sems.at[k])
        for k in range(sems.shape[0])
    ]
    for copy in copies:
        copy.start()
    for copy in copies:
        copy.wait()


def swap_leading(array, name):
    first, second, *rest = array.shape
    return pl.pallas_call(
        swap_kernel,
        out_shape=jax.ShapeDtypeStruct((second, first, *rest), array.dtype),
        in_specs=[ANYWHERE],
        out_specs=ANYWHERE,
        scratch_shapes=[pltpu.SemaphoreType.DMA((min(first, second),))],
        compiler_params=pltpu.CompilerParams(vmem_limit_bytes=2**17),
        name=name,
    )(array)


def fence_kernel(*refs):
    del refs


def fence(array, *before):
    return pl.pallas_call(
        fence_kernel,
        out_shape=jax.ShapeDtypeStruct(array.shape, array.dtype),
        in_specs=[ANYWHERE] * (1 + len(before)),
        out_specs=ANYWHERE,
        input_output_aliases={0: 0},
        compiler_params=pltpu.CompilerParams(vmem_limit_bytes=2**17),
        name="fence",
    )(array, *before)


def local(
    ensemble, obs_members, obs_value, obs_precision, tapering, routes, block_slots, block_counts
):
    mem_count = lax.axis_size("mem")
    fields, local_members, local_cells = ensemble.shape
    per_device = obs_members.shape[1] // mem_count
    owned_cells = local_cells // mem_count
    members = local_members * mem_count

    offset = lax.axis_index("mem") * per_device
    row_lists = routes[0, 0]
    targets, cap = row_lists.shape
    tiles = per_device // LANES
    both = jnp.concatenate(
        [
            lax.dynamic_slice_in_dim(obs_value, offset, per_device, 0).reshape(tiles, LANES),
            lax.dynamic_slice_in_dim(obs_precision, offset, per_device, 0).reshape(tiles, LANES),
        ],
        axis=0,
    )
    chips = targets // 2
    route_tiles = jnp.stack([row_lists >> 7, row_lists & (LANES - 1)], axis=1).astype(BF16)
    route_tiles = route_tiles.reshape(chips, 2, 2 * CAP_ROWS, LANES)
    me = lax.axis_index("pt")
    core = me & 1
    own_routes = lax.dynamic_index_in_dim(route_tiles, core, 1, keepdims=False)
    other_routes = lax.dynamic_index_in_dim(route_tiles, 1 - core, 1, keepdims=False)
    side = jnp.concatenate(
        [jnp.broadcast_to(both, (chips,) + both.shape), own_routes, other_routes], axis=1
    )

    def across(array, step):
        return lax.ppermute(array, "pt", [(p, p ^ step) for p in range(targets)])

    sides = []
    for step in range(chips):
        mine = lax.dynamic_index_in_dim(side, (me >> 1) ^ step, 0, keepdims=False)
        sides.append(across(mine, 2 * step) if step else mine)
    keep, send = scatter_taper(me.reshape(1), block_slots[0, 0], tapering[0, 0], block_counts[0, 0], targets)
    partner = across(send, 1)
    weight = spread_weights(me.reshape(1), keep, partner, sides, tiles)

    split_obs = obs_members.reshape(local_members, mem_count, per_device)
    collected = lax.all_to_all(split_obs, "mem", split_axis=1, concat_axis=1, tiled=True)
    state = ensemble.reshape(fields, local_members, mem_count, owned_cells)
    state = swap_leading(jnp.swapaxes(state, 1, 2), "outward")
    state = fence(state, partner, *sides[1:])
    collected = fence(jnp.swapaxes(collected, 0, 1), state)
    pieces = [across(collected, 2 * step) if step else collected for step in range(chips)]
    begun = gram_sums(weight, pieces[:1], sides[:1], 0)
    own, other = gram_sums(weight, pieces[1:], sides[1:], 1, begun)
    weights = solve_weights(own, across(other, 1), members)

    state = lax.all_to_all(state, "mem", split_axis=0, concat_axis=0, tiled=True)
    analysed = apply_weights(state, weights)
    returned = lax.all_to_all(analysed, "mem", split_axis=0, concat_axis=0, tiled=True)
    returned = swap_leading(returned, "homeward")
    return jnp.swapaxes(returned, 1, 2).reshape(ensemble.shape)


def solution(mesh):
    placed = (
        P(None, "mem", "pt"),
        P("mem", "pt"),
        P("pt"),
        P("pt"),
        P("pt", "mem", None, None),
        P("mem", "pt", None, None),
        P("pt", "mem", None, None),
        P("pt", "mem", None),
    )
    return jax.shard_map(
        local, mesh=mesh, in_specs=placed, out_specs=P(None, "mem", "pt"), check_vma=False
    )
```

```python
import functools
import math

import jax
import jax.numpy as jnp
from jax import lax
from jax.experimental import pallas as pl
from jax.experimental.pallas import tpu as pltpu
from jax.sharding import PartitionSpec as P

NS_ITERS = 6
LANES = 128
CHUNK = 256
GROUP = 8
CAP_SHIFT = 3
CAP_ROWS = 1 << CAP_SHIFT
F32 = jnp.float32
BF16 = jnp.bfloat16
NN = (((1,), (0,)), ((), ()))
NT = (((1,), (1,)), ((), ()))
TN = (((0,), (0,)), ((), ()))


def scatter_kernel(me_ref, slots_ref, taper_ref, counts_ref, keep_ref, send_ref):
    blocks, width = slots_ref.shape
    rows = keep_ref.shape[1]
    cap_rows = CAP_ROWS
    core = me_ref[0] & 1
    position = lax.broadcasted_iota(jnp.int32, (1, width), 1)
    hi_iota = lax.broadcasted_iota(jnp.int32, (2 * rows, LANES), 0).astype(BF16)
    lo_iota = lax.broadcasted_iota(jnp.int32, (LANES, LANES), 0).astype(BF16)
    hi_iota = jnp.concatenate([hi_iota] * (width // LANES), axis=1)
    lo_iota = jnp.concatenate([lo_iota] * (width // LANES), axis=1)
    none, one = jnp.zeros((), BF16), jnp.ones((), BF16)
    taper = taper_ref[...].astype(F32)
    for b in range(blocks):
        slots = slots_ref[b : b + 1, :]
        live = position < counts_ref[b]
        value = jnp.where(live, taper[b : b + 1, :], 0.0).astype(BF16)
        slot_row = slots >> 7
        source = slot_row >> CAP_SHIFT
        place = ((source & 1) ^ core) * rows + (source >> 1) * cap_rows + (slot_row & (cap_rows - 1))
        hi = jnp.where(hi_iota == place.astype(F32).astype(BF16), value, none)
        lo = jnp.where(lo_iota == (slots & (LANES - 1)).astype(F32).astype(BF16), one, none)
        spread = lax.dot_general(hi, lo, NT, preferred_element_type=F32)
        keep_ref[b] = spread[:rows]
        send_ref[b] = spread[rows:]


def scatter_taper(me, slots, taper, counts, sources):
    blocks = slots.shape[0]
    vmem = pl.BlockSpec(memory_space=pltpu.VMEM)
    smem = pl.BlockSpec(memory_space=pltpu.SMEM)
    half = jax.ShapeDtypeStruct((blocks, sources // 2 * CAP_ROWS, LANES), F32)
    return pl.pallas_call(
        scatter_kernel,
        out_shape=(half, half),
        in_specs=[smem, vmem, vmem, smem],
        out_specs=(vmem, vmem),
        compiler_params=pltpu.CompilerParams(vmem_limit_bytes=32 * 2**20),
        cost_estimate=pl.CostEstimate(flops=10**9, bytes_accessed=10**6, transcendentals=0),
        name="scatter_taper",
    )(me, slots, taper, counts)


def spread_kernel(me_ref, keep_ref, partner_ref, *refs):
    *side_refs, weight_ref, lhs_ref = refs
    blocks = keep_ref.shape[0]
    tiles = weight_ref.shape[2]
    parts = CAP_ROWS
    tile_iota = lax.broadcasted_iota(jnp.int32, (tiles, LANES), 0).astype(F32)
    lane_iota = lax.broadcasted_iota(jnp.int32, (LANES, LANES), 0).astype(F32)
    for step, side_ref in enumerate(side_refs):
        source = (me_ref[0] >> 1) ^ step
        precision = side_ref[tiles : 2 * tiles, :].astype(F32)
        for h, slot_ref in enumerate((keep_ref, partner_ref)):
            base = 2 * tiles + 2 * h * parts
            route = side_ref[base : base + 2 * parts, :].astype(F32)
            route_hi, route_lo = route[:parts], route[parts:]
            onehots = []
            for c in range(parts):
                onehots.append(jnp.where(lane_iota == route_lo[c : c + 1, :], 1.0, 0.0).astype(BF16))
                in_tile = tile_iota == route_hi[c : c + 1, :]
                for b in range(blocks):
                    row = slot_ref[b, pl.ds(source * parts + c, 1), :]
                    lhs_ref[b * tiles : (b + 1) * tiles, c * LANES : (c + 1) * LANES] = jnp.where(
                        in_tile, row, 0.0
                    ).astype(BF16)
            rows = lax.dot_general(
                lhs_ref[...], jnp.concatenate(onehots, axis=1), NT, preferred_element_type=F32
            )
            for b in range(blocks):
                weight_ref[step, h * blocks + b] = rows[b * tiles : (b + 1) * tiles] * precision


def spread_weights(me, keep, partner, sides, tiles):
    blocks = keep.shape[0]
    vmem = pl.BlockSpec(memory_space=pltpu.VMEM)
    smem = pl.BlockSpec(memory_space=pltpu.SMEM)
    return pl.pallas_call(
        spread_kernel,
        out_shape=jax.ShapeDtypeStruct((len(sides), 2 * blocks, tiles, LANES), F32),
        in_specs=[smem, vmem, vmem] + [vmem] * len(sides),
        out_specs=vmem,
        scratch_shapes=[pltpu.VMEM((blocks * tiles, CAP_ROWS * LANES), BF16)],
        compiler_params=pltpu.CompilerParams(vmem_limit_bytes=32 * 2**20),
        cost_estimate=pl.CostEstimate(flops=10**9, bytes_accessed=10**6, transcendentals=0),
        name="spread_weights",
    )(me, keep, partner, *sides)


def member_rows(ref, at, span):
    owners, local_members = ref.shape[0], ref.shape[-2]
    width = span.stop - span.start
    return jnp.concatenate(
        [
            ref[(slice(g, g + GROUP), *at, slice(None), span)].reshape(GROUP * local_members, width)
            for g in range(0, owners, GROUP)
        ],
        axis=0,
    )


def halves_of(x):
    high = x.astype(BF16)
    return high, (x - high.astype(F32)).astype(BF16)


def product(a, b):
    a_high, a_low = halves_of(a)
    b_high, b_low = halves_of(b)
    return lax.dot_general(
        jnp.concatenate([a_high, a_high, a_low], axis=1),
        jnp.concatenate([b_high, b_low, b_high], axis=0),
        NN,
        preferred_element_type=F32,
    )


def gram_kernel(first_piece, count, weight_ref, *refs):
    piece_refs, side_refs = refs[:count], refs[count : 2 * count]
    *before_refs, own_ref, other_ref = refs[2 * count :]
    blocks = weight_ref.shape[1]
    owners, local_members, rows = piece_refs[0].shape
    members = owners * local_members
    half = blocks * members // 2
    extra_iota = lax.broadcasted_iota(jnp.int32, (LANES - members, LANES), 0)
    for s in range(count):
        piece_ref, side_ref = piece_refs[s], side_refs[s]
        values = side_ref[: rows // LANES, :].astype(F32)
        added = None
        for part in range(rows // CHUNK):
            lhs, rhs = [], []
            for u in range(CHUNK // LANES):
                t = part * (CHUNK // LANES) + u
                widened = member_rows(piece_ref, (), slice(t * LANES, (t + 1) * LANES)).astype(F32)
                mean = jnp.sum(widened, axis=0, keepdims=True) / members
                perturbed = (widened - mean).astype(BF16)
                innovation = values[t : t + 1, :] - mean
                first = innovation.astype(BF16).astype(F32)
                rest = innovation - first
                second = rest.astype(BF16).astype(F32)
                third = rest - second
                innovations = jnp.where(
                    extra_iota == 0, first, jnp.where(extra_iota == 1, second, jnp.where(extra_iota == 2, third, 0.0))
                ).astype(BF16)
                rhs.append(jnp.concatenate([perturbed, innovations], axis=0))
                wide = perturbed.astype(F32)
                lhs.append(
                    jnp.concatenate(
                        [(wide * weight_ref[first_piece + s, b, t : t + 1, :]).astype(BF16) for b in range(blocks)], axis=0
                    )
                )
            term = lax.dot_general(
                jnp.concatenate(lhs, axis=1), jnp.concatenate(rhs, axis=1), NT, preferred_element_type=F32
            )
            added = term if added is None else added + term
        for at, ref in enumerate((own_ref, other_ref)):
            term = added[at * half : (at + 1) * half]
            if s:
                ref[...] += term
            elif before_refs:
                ref[...] = before_refs[at][...] + term
            else:
                ref[...] = term


def gram_sums(weight, pieces, sides, first_piece, before=()):
    blocks = weight.shape[1]
    owners, local_members, _ = pieces[0].shape
    vmem = pl.BlockSpec(memory_space=pltpu.VMEM)
    sums = jax.ShapeDtypeStruct((blocks // 2 * owners * local_members, LANES), F32)
    return pl.pallas_call(
        functools.partial(gram_kernel, first_piece, len(pieces)),
        out_shape=(sums, sums),
        in_specs=[vmem] * (1 + len(pieces) + len(sides) + len(before)),
        out_specs=(vmem, vmem),
        compiler_params=pltpu.CompilerParams(vmem_limit_bytes=32 * 2**20),
        cost_estimate=pl.CostEstimate(flops=len(pieces) * 2 * 10**9, bytes_accessed=10**6, transcendentals=0),
        name="gram_sums",
    )(weight, *pieces, *sides, *before)


def solve_kernel(own_ref, other_ref, out_ref):
    pairs, twice, _ = out_ref.shape
    members = twice // 2
    row = lax.broadcasted_iota(jnp.int32, (twice, twice), 0)
    column = lax.broadcasted_iota(jnp.int32, (twice, twice), 1)
    identity = jnp.where(row == column, 1.0, 0.0)
    same = (row < members) == (column < members)
    upper = lax.broadcasted_iota(jnp.int32, (twice, 1), 0) < members
    halves, scales, projections = [], [], []
    for p in range(pairs):
        total = own_ref[p * twice : (p + 1) * twice, :] + other_ref[p * twice : (p + 1) * twice, :]
        projections.append(jnp.sum(jnp.where(column < members, 0.0, total), axis=1, keepdims=True))
        shifted = pltpu.roll(total[members:], members, 1)
        gram = jnp.where(same, jnp.concatenate([total[:members], shifted], axis=0), 0.0)
        system = (members - 1.0) * identity + 0.5 * (gram + gram.T)
        squares = jnp.sum(system * system, axis=1, keepdims=True)
        frobenius = jnp.sqrt(
            jnp.where(
                upper,
                jnp.sum(jnp.where(upper, squares, 0.0), keepdims=True),
                jnp.sum(jnp.where(upper, 0.0, squares), keepdims=True),
            )
        )
        halves.append(system / frobenius)
        scales.append(jnp.sqrt(frobenius))
    inverses = []
    for sweep in range(NS_ITERS):
        updates = [
            1.5 * identity - 0.5 * (product(inverses[p], halves[p]) if sweep else halves[p]) for p in range(pairs)
        ]
        if sweep == 0:
            halves = [product(halves[p], updates[p]) for p in range(pairs)]
            inverses = updates
        elif sweep < NS_ITERS - 1:
            both = [product(jnp.concatenate([halves[p], inverses[p]], axis=0), updates[p]) for p in range(pairs)]
            halves = [x[:twice] for x in both]
            inverses = [x[twice:] for x in both]
        else:
            inverses = [product(inverses[p], updates[p]) for p in range(pairs)]
    for p in range(pairs):
        inverse_root = inverses[p] / scales[p]
        inner = jnp.sum(inverse_root * projections[p], axis=0, keepdims=True)
        mean_shift = jnp.sum(inverse_root * inner, axis=1, keepdims=True)
        out_ref[p] = jnp.where(same, math.sqrt(members - 1.0) * inverse_root + mean_shift, 0.0).astype(BF16)


def solve_weights(own, other, members):
    vmem = pl.BlockSpec(memory_space=pltpu.VMEM)
    twice = 2 * members
    return pl.pallas_call(
        solve_kernel,
        out_shape=jax.ShapeDtypeStruct((own.shape[0] // twice, twice, twice), BF16),
        in_specs=[vmem, vmem],
        out_specs=vmem,
        compiler_params=pltpu.CompilerParams(vmem_limit_bytes=32 * 2**20),
        cost_estimate=pl.CostEstimate(flops=3 * 10**9, bytes_accessed=10**6, transcendentals=0),
        name="solve_weights",
    )(own, other)


def apply_kernel(state_ref, weights_ref, out_ref):
    owners, fields, local_members, cells = state_ref.shape
    members = owners * local_members
    pairs, twice, _ = weights_ref.shape
    size = cells // (2 * pairs)
    for f in range(fields):
        for p in range(pairs):
            spans = [slice((2 * p + h) * size, (2 * p + h + 1) * size) for h in range(2)]
            means, deviations = [], []
            for span in spans:
                widened = member_rows(state_ref, (f,), span).astype(F32)
                mean = jnp.sum(widened, axis=0, keepdims=True) / members
                means.append(mean)
                deviations.append((widened - mean).astype(BF16))
            moved = lax.dot_general(
                weights_ref[p], jnp.concatenate(deviations, axis=0), TN, preferred_element_type=F32
            )
            for h, span in enumerate(spans):
                out_ref[:, f, :, span] = (
                    (means[h] + moved[h * members : (h + 1) * members]).astype(BF16).reshape(owners, local_members, size)
                )


def apply_weights(state, weights):
    vmem = pl.BlockSpec(memory_space=pltpu.VMEM)
    return pl.pallas_call(
        apply_kernel,
        out_shape=jax.ShapeDtypeStruct(state.shape, BF16),
        in_specs=[vmem, vmem],
        out_specs=vmem,
        compiler_params=pltpu.CompilerParams(vmem_limit_bytes=32 * 2**20),
        cost_estimate=pl.CostEstimate(flops=10**9, bytes_accessed=2 * 10**6, transcendentals=0),
        name="apply_weights",
    )(state, weights)


ANYWHERE = pl.BlockSpec(memory_space=pl.ANY)


def swap_kernel(from_ref, to_ref, sems):
    copies = [
        pltpu.make_async_copy(from_ref.at[:, k], to_ref.at[k], sems.at[k])
        if from_ref.shape[0] > from_ref.shape[1]
        else pltpu.make_async_copy(from_ref.at[k], to_ref.at[:, k], sems.at[k])
        for k in range(sems.shape[0])
    ]
    for copy in copies:
        copy.start()
    for copy in copies:
        copy.wait()


def swap_leading(array, name):
    first, second, *rest = array.shape
    return pl.pallas_call(
        swap_kernel,
        out_shape=jax.ShapeDtypeStruct((second, first, *rest), array.dtype),
        in_specs=[ANYWHERE],
        out_specs=ANYWHERE,
        scratch_shapes=[pltpu.SemaphoreType.DMA((min(first, second),))],
        compiler_params=pltpu.CompilerParams(vmem_limit_bytes=2**17),
        name=name,
    )(array)


def fence_kernel(*refs):
    del refs


def fence(array, *before):
    return pl.pallas_call(
        fence_kernel,
        out_shape=jax.ShapeDtypeStruct(array.shape, array.dtype),
        in_specs=[ANYWHERE] * (1 + len(before)),
        out_specs=ANYWHERE,
        input_output_aliases={0: 0},
        compiler_params=pltpu.CompilerParams(vmem_limit_bytes=2**17),
        name="fence",
    )(array, *before)


def local(
    ensemble, obs_members, obs_value, obs_precision, tapering, routes, block_slots, block_counts
):
    mem_count = lax.axis_size("mem")
    fields, local_members, local_cells = ensemble.shape
    per_device = obs_members.shape[1] // mem_count
    owned_cells = local_cells // mem_count
    members = local_members * mem_count

    offset = lax.axis_index("mem") * per_device
    row_lists = routes[0, 0]
    targets, cap = row_lists.shape
    tiles = per_device // LANES
    both = jnp.concatenate(
        [
            lax.dynamic_slice_in_dim(obs_value, offset, per_device, 0).reshape(tiles, LANES),
            lax.dynamic_slice_in_dim(obs_precision, offset, per_device, 0).reshape(tiles, LANES),
        ],
        axis=0,
    )
    chips = targets // 2
    route_tiles = jnp.stack([row_lists >> 7, row_lists & (LANES - 1)], axis=1).astype(BF16)
    route_tiles = route_tiles.reshape(chips, 2, 2 * CAP_ROWS, LANES)
    me = lax.axis_index("pt")
    core = me & 1
    own_routes = lax.dynamic_index_in_dim(route_tiles, core, 1, keepdims=False)
    other_routes = lax.dynamic_index_in_dim(route_tiles, 1 - core, 1, keepdims=False)
    side = jnp.concatenate(
        [jnp.broadcast_to(both, (chips,) + both.shape), own_routes, other_routes], axis=1
    )

    def across(array, step):
        return lax.ppermute(array, "pt", [(p, p ^ step) for p in range(targets)])

    sides = []
    for step in range(chips):
        mine = lax.dynamic_index_in_dim(side, (me >> 1) ^ step, 0, keepdims=False)
        sides.append(across(mine, 2 * step) if step else mine)
    keep, send = scatter_taper(me.reshape(1), block_slots[0, 0], tapering[0, 0], block_counts[0, 0], targets)

    split_obs = obs_members.reshape(local_members, mem_count, per_device)
    collected = lax.all_to_all(split_obs, "mem", split_axis=1, concat_axis=1, tiled=True)
    state = ensemble.reshape(fields, local_members, mem_count, owned_cells)
    state = swap_leading(jnp.swapaxes(state, 1, 2), "outward")
    state = fence(state, send, *sides[1:])
    collected = fence(jnp.swapaxes(collected, 0, 1), state)
    pieces = [across(collected, 2 * step) if step else collected for step in range(chips)]
    partner = across(fence(send, collected), 1)
    weight = spread_weights(me.reshape(1), keep, partner, sides, tiles)
    begun = gram_sums(weight, pieces[:1], sides[:1], 0)
    own, other = gram_sums(weight, pieces[1:], sides[1:], 1, begun)
    weights = solve_weights(own, across(other, 1), members)

    state = lax.all_to_all(state, "mem", split_axis=0, concat_axis=0, tiled=True)
    analysed = apply_weights(state, weights)
    returned = lax.all_to_all(analysed, "mem", split_axis=0, concat_axis=0, tiled=True)
    returned = swap_leading(returned, "homeward")
    return jnp.swapaxes(returned, 1, 2).reshape(ensemble.shape)


def solution(mesh):
    placed = (
        P(None, "mem", "pt"),
        P("mem", "pt"),
        P("pt"),
        P("pt"),
        P("pt", "mem", None, None),
        P("mem", "pt", None, None),
        P("pt", "mem", None, None),
        P("pt", "mem", None),
    )
    return jax.shard_map(
        local, mesh=mesh, in_specs=placed, out_specs=P(None, "mem", "pt"), check_vma=False
    )
```
